128 devices in a mesh: row: 32 (over y, x_lo, z), col: 4 (over x_hi, core).
Axes of the slice: x: 4 (x_hi: 2, x_lo: 2; x = x_hi * 2 + x_lo), y: 4, z: 4, core: 2. Of those that a mesh axis runs over, the one named last changes fastest.
Arguments:
- tokens: bfloat16 [16384, 2048], P('row', 'col'), may hold values from -6 to 6
- w_query: bfloat16 [2048, 2048], P('row', 'col'), may hold values from -0.125 to 0.125
- key_value_weight: bfloat16 [2048, 512], P('row', 'col'), may hold values from -0.125 to 0.125
- w_output: bfloat16 [2048, 2048], P('col', 'row'), may hold values from -0.5 to 0.5
- w_gate: bfloat16 [2048, 5632], P('row', 'col'), may hold values from -0.125 to 0.125
- w_up: bfloat16 [2048, 5632], P('row', 'col'), may hold values from -0.125 to 0.125
- w_down: bfloat16 [5632, 2048], P('col', 'row'), may hold values from -0.078125 to 0.078125
- gain_attention: bfloat16 [2048], P('row'), may hold values from 0.5 to 1.5
- gain_mlp: bfloat16 [2048], P('row'), may hold values from 0.5 to 1.5
- segment: int32 [16384], P('row'), may hold values from 0 to 8, as said below
- position: int32 [16384], P('row'), may hold values from 0 to 511, as said below
- cotangent: bfloat16 [16384, 2048], P('row', 'col'), may hold values from -6 to 6
Outputs:
- mixed: bfloat16 [16384, 2048], P('row', 'col')
- input_grad: float32 [16384, 2048], P('row', 'col')
- grad_query: float32 [2048, 2048], P('row', 'col')
- grad_keyval: float32 [2048, 512], P('row', 'col')
- grad_output: float32 [2048, 2048], P('col', 'row')
- grad_gate: float32 [2048, 5632], P('row', 'col')
- grad_up: float32 [2048, 5632], P('row', 'col')
- grad_down: float32 [5632, 2048], P('col', 'row')
- grad_gain_attention: float32 [2048], P('row')
- grad_gain_mlp: float32 [2048], P('row')
The draws below stay inside these ranges and needn't reach their ends.
Inputs may be any that keep to these rules, and one draw needn't show every extreme that they name: `segment`: within each sequence of 512 tokens document numbers start at 0 and rise by one at each document's first token; every document holds 60 to min(800, 512) tokens, except the last of a sequence, which is cut at the sequence's end. `position`: A token's place counted from its document's first token.
All inputs are finite; a program needn't handle non-finite values.
Results may differ from the reference program's by a relative error of at most 0.029.
Values may be sent and summed in bfloat16 or wider, within the bound.
No kernel may reach another device: no remote copies, remote signals or barrier semaphores. Data moves between devices by JAX's collectives and lax.ppermute only.
A program may use at most 128 MiB of HBM per device.

```python
import math
import jax
import jax.numpy as jnp
from jax import lax

MODEL_WIDTH = 2048
QUERY_HEADS = 32
KEY_VALUE_HEADS = 4
HEAD_SIZE = 64
FF = 5632
TOKENS_PER_ROW = 512
DOC_MIN = 60
DOC_MAX = 800
TOKENS = 16384


def layout(key):
    doc_slots = TOKENS_PER_ROW // DOC_MIN + 1
    longest = min(DOC_MAX, TOKENS_PER_ROW)
    sequence_count = TOKENS // TOKENS_PER_ROW
    length_key, long_key, short_key = jax.random.split(key, 3)
    drawn = jax.random.randint(length_key, (sequence_count, doc_slots), DOC_MIN, longest + 1).astype(jnp.int32)
    long_seq = jax.random.randint(long_key, (), 0, sequence_count).astype(jnp.int32)
    short_seq = ((long_seq + jax.random.randint(short_key, (), 1, sequence_count).astype(jnp.int32)) % sequence_count).astype(jnp.int32)
    seq_number = jnp.arange(sequence_count).astype(jnp.int32)[:, None]
    slot_number = jnp.arange(doc_slots).astype(jnp.int32)[None, :]
    drawn = jnp.where(seq_number == short_seq, DOC_MIN, drawn).astype(jnp.int32)
    lengths = jnp.where((seq_number == long_seq) & (slot_number == 0), longest, drawn).astype(jnp.int32)
    starts = jnp.cumsum(lengths, 1).astype(jnp.int32) - lengths
    token_place = jnp.arange(TOKENS_PER_ROW).astype(jnp.int32)
    begun = starts[:, None, :] <= token_place[None, :, None]
    doc_ids = jnp.sum(begun.astype(jnp.int32), -1).astype(jnp.int32) - 1
    first_token = jnp.max(jnp.where(begun, starts[:, None, :], 0), -1).astype(jnp.int32)
    places = token_place[None, :] - first_token
    return (doc_ids.reshape(-1).astype(jnp.int32), places.reshape(-1).astype(jnp.int32))


def draw_segment(key, part):
    doc_ids, places = layout(key)
    return doc_ids


def draw_position(key, part):
    doc_ids, places = layout(key)
    return places


def level_of(rng, dims, shards, smallest, top_value):
    factor_of = 1.0
    for dim, parts in shards:
        steps = jax.random.uniform(jax.random.fold_in(jax.random.fold_in(rng, 6), dim), (parts,), jnp.float32, smallest / len(shards), top_value / len(shards))
        factor_of = factor_of * jnp.repeat(jnp.exp(steps), dims[dim] // parts).reshape((-1,) + (1,) * (len(dims) - 1 - dim))
    return factor_of


def bell_draw(rng, dims, width, most, pieces=(), kind=jnp.bfloat16):
    gain = level_of(rng, dims, pieces, -0.22, 0.18) if pieces else 1.0
    values = jax.random.normal(rng, dims, jnp.float32) * width * gain
    return jnp.minimum(jnp.maximum(values, -most), most).astype(kind)


def setup_inputs(seed: int = 0) -> dict:
    key_list = jax.random.split(jax.random.key(seed), 13)
    tokens = bell_draw(key_list[0], (TOKENS, MODEL_WIDTH), 1.0, 6.0, ((0, 32), (1, 4)))
    w_query = bell_draw(key_list[1], (MODEL_WIDTH, QUERY_HEADS * HEAD_SIZE), MODEL_WIDTH ** -0.5, 0.125, ((0, 32), (1, 4)))
    key_value_weight = bell_draw(key_list[2], (MODEL_WIDTH, 2 * KEY_VALUE_HEADS * HEAD_SIZE), MODEL_WIDTH ** -0.5, 0.125, ((0, 32), (1, 4)))
    w_output = bell_draw(key_list[3], (QUERY_HEADS * HEAD_SIZE, MODEL_WIDTH), (QUERY_HEADS * HEAD_SIZE // 16) ** -0.5, 0.5, ((0, 4), (1, 32)))
    w_gate = bell_draw(key_list[4], (MODEL_WIDTH, FF), MODEL_WIDTH ** -0.5, 0.125, ((0, 32), (1, 4)))
    w_up = bell_draw(key_list[5], (MODEL_WIDTH, FF), MODEL_WIDTH ** -0.5, 0.125, ((0, 32), (1, 4)))
    w_down = bell_draw(key_list[6], (FF, MODEL_WIDTH), FF ** -0.5, 0.078125, ((0, 4), (1, 32)))
    gain_attention = jnp.clip(1.0 + 0.1 * jax.random.normal(key_list[7], (MODEL_WIDTH,), jnp.float32), 0.5, 1.5).astype(jnp.bfloat16)
    gain_mlp = jnp.clip(1.0 + 0.1 * jax.random.normal(key_list[8], (MODEL_WIDTH,), jnp.float32), 0.5, 1.5).astype(jnp.bfloat16)
    segment = draw_segment(jax.random.fold_in(key_list[12], 71), 0)
    position = draw_position(jax.random.fold_in(key_list[12], 71), 0)
    cotangent = bell_draw(key_list[11], (TOKENS, MODEL_WIDTH), 1.0, 6.0, ((0, 32), (1, 4)))
    return {"tokens": tokens, "w_query": w_query, "key_value_weight": key_value_weight, "w_output": w_output, "w_gate": w_gate, "w_up": w_up, "w_down": w_down, "gain_attention": gain_attention, "gain_mlp": gain_mlp, "segment": segment, "position": position, "cotangent": cotangent}


@jax.custom_vjp
def low(v):
    return lax.optimization_barrier(v.astype(jnp.bfloat16)).astype(jnp.float32)

@jax.custom_vjp
def low_back(v):
    return v

def low_keep(v):
    return (low(v), None)

def low_pass(kept, grad):
    return (grad,)

def back_keep(v):
    return (v, None)

def back_low(kept, grad):
    return (low(grad),)
low.defvjp(low_keep, low_pass)
low_back.defvjp(back_keep, back_low)
EPSILON = 1e-05

def product(left, right):
    return jnp.dot(left, right, precision=lax.Precision.HIGHEST, preferred_element_type=jnp.float32)

def rotate(values, position):
    half_width = HEAD_SIZE // 2
    steps_index = jnp.arange(half_width).astype(jnp.float32)
    frequency = jnp.exp(steps_index * (-2.0 * math.log(10000.0) / HEAD_SIZE))
    angles = position.astype(jnp.float32)[:, None, None] * frequency[None, None, :]
    cosine_table = jnp.cos(angles)
    sine_table = jnp.sin(angles)
    first = values[..., :half_width]
    second = values[..., half_width:]
    return jnp.concatenate([first * cosine_table - second * sine_table, second * cosine_table + first * sine_table], -1)

def attention_block(operands):
    queries, keys, values, doc_ids = operands
    length = doc_ids.shape[0]
    raw_scores = jnp.einsum('qkgd,tkd->kgqt', queries, keys, precision=lax.Precision.HIGHEST)
    scores = low_back(raw_scores * (1.0 / math.sqrt(HEAD_SIZE)))
    token_place = jnp.arange(length)
    allowed = (doc_ids[:, None] == doc_ids[None, :]) & (token_place[:, None] >= token_place[None, :])
    masked = jnp.where(allowed, scores, -1e+30)
    row_top = lax.optimization_barrier(jnp.max(masked, -1, keepdims=True))
    exponent_terms = jnp.exp(masked - row_top)
    attn_probs = exponent_terms / lax.optimization_barrier(jnp.sum(exponent_terms, -1, keepdims=True))
    return jnp.einsum('kgqt,tkd->qkgd', low(attn_probs), values, precision=lax.Precision.HIGHEST)

def run_layer(x_float, w_query, key_value_weight, w_output, w_gate, w_up, w_down, gain_one, gain_two, segment, position):
    token_total_count = x_float.shape[0]
    sequence_count = token_total_count // TOKENS_PER_ROW
    group_width = QUERY_HEADS // KEY_VALUE_HEADS
    rms_one = lax.rsqrt(lax.optimization_barrier(jnp.mean(x_float * x_float, -1, keepdims=True)) + EPSILON)
    normed_one = low(x_float * rms_one * gain_one)
    query_proj = low_back(product(normed_one, w_query))
    key_value_projected = low_back(product(normed_one, key_value_weight))
    query_heads = query_proj.reshape(token_total_count, QUERY_HEADS, HEAD_SIZE)
    key_value_heads = key_value_projected.reshape(token_total_count, KEY_VALUE_HEADS, 2, HEAD_SIZE)
    rotated_query = low(rotate(query_heads, position))
    rotated_key = low(rotate(key_value_heads[:, :, 0], position))
    value_reduced = low(key_value_heads[:, :, 1])
    attended_rows = lax.map(jax.checkpoint(attention_block), (rotated_query.reshape(sequence_count, TOKENS_PER_ROW, KEY_VALUE_HEADS, group_width, HEAD_SIZE), rotated_key.reshape(sequence_count, TOKENS_PER_ROW, KEY_VALUE_HEADS, HEAD_SIZE), value_reduced.reshape(sequence_count, TOKENS_PER_ROW, KEY_VALUE_HEADS, HEAD_SIZE), segment.reshape(sequence_count, TOKENS_PER_ROW)))
    attended_rows = low(low_back(attended_rows.reshape(token_total_count, QUERY_HEADS * HEAD_SIZE)))
    resid = x_float + low_back(product(attended_rows, w_output))
    rms_two = lax.rsqrt(lax.optimization_barrier(jnp.mean(resid * resid, -1, keepdims=True)) + EPSILON)
    normed_two = low(resid * rms_two * gain_two)
    gate_value = low_back(product(normed_two, w_gate))
    up_value = low_back(product(normed_two, w_up))
    activated = low(gate_value * jax.nn.sigmoid(gate_value) * up_value)
    return resid + product(activated, w_down)

def reference(tokens, w_query, key_value_weight, w_output, w_gate, w_up, w_down, gain_attention, gain_mlp, segment, position, cotangent):
    floats = [a.astype(jnp.float32) for a in (tokens, w_query, key_value_weight, w_output, w_gate, w_up, w_down, gain_attention, gain_mlp)]

    def layer_only(*arrays):
        return run_layer(*arrays, segment, position)
    result, pullback = jax.vjp(layer_only, *floats)
    grads = pullback(cotangent.astype(jnp.float32))
    return (result.astype(jnp.bfloat16), grads[0], grads[1], grads[2], grads[3], grads[4], grads[5], grads[6], grads[7], grads[8])
```

```python
import math

import jax
import jax.numpy as jnp
from jax import lax
from jax.experimental import pallas as pl
from jax.experimental.pallas import tpu as pltpu
from jax.sharding import Mesh, PartitionSpec as P

F32, BF16 = jnp.float32, jnp.bfloat16
HEAD = 64
HALF = HEAD // 2
EPSILON = 1e-05
MASKED = -1e30
AXES = ("y", "xl", "z", "xh", "core")
SIZES = (4, 2, 4, 2, 2)
ROW, COL = ("y", "xl", "z"), ("xh", "core")

SEQ = 512
BOTH = 2 * SEQ
MODEL = 2048
BLOCK = 512
QROWS = 512
QKV = QROWS + 128
GAINS_AT = QKV + 512
GAINS = 32
FFN = 704
VMEM = 56 * 1024 * 1024


def turn(second, mask):
    pairs = []
    for i in range(32):
        shift = 1 if (i % 2 == 0) != second else 3
        pairs.append((i, i ^ (mask << shift)))
    return lambda v: lax.ppermute(v, ("y", "z", "core"), pairs)


def cross(second):
    pairs = []
    for i in range(8):
        near = (i % 2 == 0) != second
        pairs.append((i, i ^ (4 if near else 6)))
    return lambda v: lax.ppermute(v, ("xl", "xh", "core"), pairs)


def swap_core(v):
    return lax.ppermute(v, "core", [(0, 1), (1, 0)])


def swap_xh(v):
    return lax.ppermute(v, "xh", [(0, 1), (1, 0)])


def swap_xl(v):
    return lax.ppermute(v, "xl", [(0, 1), (1, 0)])


def narrow(v):
    return v.astype(BF16)


def wide(v):
    return v.astype(F32)


def gather_ring(v, near, far):
    half = v.shape[0] // 2
    from_near, from_far = near(v), far(v)
    return v, from_near, far(from_near[:half]), near(from_far[half:]), from_far


def gather_two(v):
    held = jnp.concatenate(gather_ring(v, turn(False, 1), turn(False, 3)), 0)
    return gather_ring(held.reshape(4, *v.shape), turn(True, 1), turn(True, 3))


def reduce_two(terms):
    low, high, one, three, own = terms
    near, far = turn(True, 1), turn(True, 3)
    three = add_into(three, near(low), 0)
    one = add_into(one, far(high), 2)
    held = narrow(wide(own) + wide(near(one)) + wide(far(three)))
    near, far = turn(False, 1), turn(False, 3)
    half = held.shape[1] // 2
    to_near = near(held[2, :half])
    to_far = far(held[2, half:])
    third = jnp.concatenate([narrow(wide(held[3, :half]) + wide(to_near)), held[3, half:]], 0)
    first = jnp.concatenate([held[1, :half], narrow(wide(held[1, half:]) + wide(to_far))], 0)
    return wide(held[0]) + wide(near(first)) + wide(far(third))


def dot(a, b, contract):
    return lax.dot_general(a, b, ((contract[:1], contract[1:]), ((), ())), preferred_element_type=F32)


def nn(a, b):
    return dot(a, b, (1, 0))


def nt(a, b):
    return dot(a, b, (1, 1))


def tn(a, b):
    return dot(a, b, (0, 0))


def params():
    return pltpu.CompilerParams(vmem_limit_bytes=VMEM)


def spec(shape, index=None):
    zeros = (0,) * len(shape)
    return pl.BlockSpec(shape, index if index is not None else (lambda *_: zeros))


def whole(*arrays):
    return [spec(a.shape) for a in arrays]


def out(*shape, dtype=BF16):
    return jax.ShapeDtypeStruct(shape, dtype)


def lane_low(shape):
    return lax.broadcasted_iota(jnp.int32, shape, 1) < 64


def pair(a, b):
    low = lane_low(a.shape)
    return jnp.where(low, a, pltpu.roll(b, 64, 1)), jnp.where(low, pltpu.roll(a, 64, 1), b)


def to_inner_kernel(a_ref, b_ref, c_ref, d_ref):
    for src, dst in ((a_ref, c_ref), (b_ref, d_ref)):
        t = [wide(src[:, k * 128 : (k + 1) * 128]) for k in range(4)]
        z0, z1 = pair(t[0], t[2])
        z2, z3 = pair(t[1], t[3])
        for k, value in enumerate((z0, z1, z2, z3)):
            dst[:, k * 128 : (k + 1) * 128] = narrow(value)


def to_inner(a, b):
    return pl.pallas_call(
        to_inner_kernel, out_shape=(out(*a.shape), out(*b.shape)), compiler_params=params()
    )(a, b)


def to_natural(v):
    z = [v[:, k * 128 : (k + 1) * 128] for k in range(4)]
    t0, t2 = pair(z[0], z[1])
    t1, t3 = pair(z[2], z[3])
    return jnp.concatenate([t0, t1, t2, t3], 1)


def fetch(table, blocks, target, sems, start, to=0):
    own, one, low, high, three = blocks
    rows = target.shape[0]
    copies = []
    for j in range(4):
        for i in range(4):
            if j == 2:
                src = low.at[i] if i < 2 else high.at[i - 2]
            else:
                src = (own, one, None, three)[j].at[i]
            lanes = pl.multiple_of(table[4 * j + i], 128)
            copy = pltpu.make_async_copy(
                src.at[pl.ds(start, rows)], target.at[:, pl.ds(lanes, 128)], sems.at[to + len(copies)]
            )
            copy.start()
            copies.append(copy)
    return copies


def wait(copies):
    for copy in copies:
        copy.wait()


ANYWHERE = pl.BlockSpec(memory_space=pl.ANY)
SCALARS = pl.BlockSpec(memory_space=pltpu.SMEM)


def add_into_kernel(a, b, a_o):
    a_o[...] = narrow(wide(a[...]) + wide(b[...]))


def add_into(a, b, start):
    block = (1,) + a.shape[1:]
    return pl.pallas_call(
        add_into_kernel,
        grid=(2,),
        in_specs=[spec(block, lambda i: (start + i, 0, 0)), spec(block, lambda i: (i, 0, 0))],
        out_specs=spec(block, lambda i: (start + i, 0, 0)),
        out_shape=out(*a.shape),
        input_output_aliases={0: 0},
        compiler_params=params(),
    )(a, b)


def rotated(v, cos, sin):
    a, b = v[:HALF], v[HALF:]
    return jnp.concatenate([a * cos - b * sin, b * cos + a * sin], 0)


def rotated_back(v, cos, sin):
    a, b = v[:HALF], v[HALF:]
    return jnp.concatenate([a * cos + b * sin, b * cos - a * sin], 0)


def project_kernel(table, x0, x1, x2, x3, cos, sin, *refs):
    blocks, (x_o, n_o, r_o, q_o, k_o, v_o, gains_o, w, gains, sems) = refs[:5], refs[5:]

    @pl.when(pl.program_id(0) == 0)
    def _():
        copies = fetch(table, blocks, w, sems, 0) + fetch(table, blocks, gains, sems, GAINS_AT, 16)
        wait(copies)
        gains_o[...] = gains[...]

    x_low = jnp.concatenate([x0[...], x1[...], x2[...], x3[...]], 1)
    x_o[...] = x_low
    x = wide(x_low)
    r = lax.rsqrt(jnp.mean(x * x, -1, keepdims=True) + EPSILON)
    r_o[...] = r
    normed = narrow(x * r * wide(gains[0:1, :]))
    n_o[...] = normed
    qkv = nt(w[...], normed)
    c, s = cos[...], sin[...]
    for h in range(QROWS // HEAD):
        q_o[h * HEAD : (h + 1) * HEAD, :] = narrow(rotated(qkv[h * HEAD : (h + 1) * HEAD], c, s))
    k_o[...] = narrow(rotated(qkv[QROWS : QROWS + HEAD], c, s))
    v_o[...] = narrow(qkv[QROWS + HEAD :])


def project(table, x, blocks, cos, sin):
    t = 256
    row = lambda i: (i, 0)
    lane = lambda i: (0, i)
    return pl.pallas_call(
        project_kernel,
        grid=(SEQ // t,),
        in_specs=[SCALARS] + [spec((t, BLOCK), row)] * 4 + [spec((HALF, t), lane)] * 2 + [ANYWHERE] * 5,
        out_specs=(
            spec((t, MODEL), row),
            spec((t, MODEL), row),
            spec((t, 1), row),
            spec((QROWS, t), lane),
            spec((HEAD, t), lane),
            spec((HEAD, t), lane),
            spec((GAINS, MODEL)),
        ),
        out_shape=(
            out(SEQ, MODEL),
            out(SEQ, MODEL),
            out(SEQ, 1, dtype=F32),
            out(QROWS, SEQ),
            out(HEAD, SEQ),
            out(HEAD, SEQ),
            out(GAINS, MODEL),
        ),
        scratch_shapes=[
            pltpu.VMEM((QKV, MODEL), BF16),
            pltpu.VMEM((GAINS, MODEL), BF16),
            pltpu.SemaphoreType.DMA((32,)),
        ],
        compiler_params=params(),
    )(table, *x, cos, sin, *blocks)


def attend_kernel(q, k, v, seg_row, seg_col, o_o, p_o):
    s = tn(k[...], q[...]) * (1.0 / math.sqrt(HEAD))
    shape = (SEQ, SEQ)
    key = lax.broadcasted_iota(jnp.int32, shape, 0)
    query = lax.broadcasted_iota(jnp.int32, shape, 1)
    allowed = (seg_col[...] == seg_row[...]) & (key <= query)
    s = jnp.where(allowed, s, MASKED)
    e = jnp.exp(s - jnp.max(s, 0, keepdims=True))
    p = narrow(e * (1.0 / jnp.sum(e, 0, keepdims=True)))
    p_o[0] = p
    o_o[...] = narrow(nn(v[...], p))


def attend(q, k, v, seg_row, seg_col):
    heads = QROWS // HEAD
    head = lambda h: (h, 0)
    return pl.pallas_call(
        attend_kernel,
        grid=(heads,),
        in_specs=[spec((HEAD, SEQ), head)] + whole(k, v, seg_row, seg_col),
        out_specs=(spec((HEAD, SEQ), head), spec((1, SEQ, SEQ), lambda h: (h, 0, 0))),
        out_shape=(out(QROWS, SEQ), out(heads, SEQ, SEQ)),
        compiler_params=params(),
    )(q, k, v, seg_row, seg_col)


def out_project_kernel(table, o, *refs):
    blocks, (keep_o, send_o, w, sems) = refs[:5], refs[5:]
    wait(fetch(table, blocks, w, sems, QKV))
    for k in range(2):
        value = tn(o[...], w[:, 2 * k * BLOCK : (2 * k + 2) * BLOCK])
        keep_o[k] = narrow(value[:, :BLOCK])
        send_o[k] = narrow(value[:, BLOCK:])


def out_project(table, o, blocks):
    return pl.pallas_call(
        out_project_kernel,
        in_specs=[SCALARS] + [spec(o.shape)] + [ANYWHERE] * 5,
        out_specs=(spec((2, SEQ, BLOCK)),) * 2,
        out_shape=(out(2, SEQ, BLOCK),) * 2,
        scratch_shapes=[pltpu.VMEM((QROWS, MODEL), BF16), pltpu.SemaphoreType.DMA((16,))],
        compiler_params=params(),
    )(table, o, *blocks)


def put_chunks(value, where, keep_o, send_o):
    for k in range(2):
        keep_o[where[4] ^ k] = narrow(value[:, 2 * k * BLOCK : (2 * k + 1) * BLOCK])
        send_o[where[5] ^ k] = narrow(value[:, (2 * k + 1) * BLOCK : (2 * k + 2) * BLOCK])


def mlp_kernel(table, where, *refs):
    h_in, cot_in, (gains,), blocks, refs = refs[:4], refs[4:8], refs[8:9], refs[9:14], refs[14:]
    n_o, r_o, h_o, cot_o, act_o, dg_o, du_o, keep_o, send_o, wg, wu, wd, sems = refs

    @pl.when(pl.program_id(0) == 0)
    def _():
        copies = []
        for k, w in enumerate((wg, wu, wd)):
            copies += fetch(table, blocks, w, sems, k * FFN, 16 * k)
        wait(copies)

    for k in range(4):
        lanes = pl.ds(pl.multiple_of(where[k], BLOCK), BLOCK)
        h_o[:, lanes] = h_in[k][...]
        cot_o[:, lanes] = cot_in[k][...]
    hidden = wide(h_o[...])
    r = lax.rsqrt(jnp.mean(hidden * hidden, -1, keepdims=True) + EPSILON)
    r_o[...] = r
    normed = narrow(hidden * r * wide(gains[1:2, :]))
    n_o[...] = normed
    gate = nt(wg[...], normed)
    up = nt(wu[...], normed)
    d_act = nt(wd[...], cot_o[...])
    g = jax.nn.sigmoid(gate)
    silu = gate * g
    act_o[...] = narrow(silu * up)
    d_up = narrow(d_act * silu)
    d_gate = narrow(d_act * up * (g + silu * (1.0 - g)))
    dg_o[...] = d_gate
    du_o[...] = d_up
    put_chunks(tn(d_gate, wg[...]) + tn(d_up, wu[...]), where, keep_o, send_o)


def mlp(table, where, h, cot, gains, blocks):
    t = 256
    row = lambda i: (i, 0)
    part = spec((t, BLOCK), row)
    chunk = spec((2, t, BLOCK), lambda i: (0, i, 0))
    hid = spec((FFN, t), lambda i: (0, i))
    full = spec((t, MODEL), row)
    return pl.pallas_call(
        mlp_kernel,
        grid=(SEQ // t,),
        in_specs=[SCALARS] * 2 + [part] * 8 + whole(gains) + [ANYWHERE] * 5,
        out_specs=(full, spec((t, 1), row), full, full, hid, hid, hid, chunk, chunk),
        out_shape=(
            out(SEQ, MODEL),
            out(SEQ, 1, dtype=F32),
            out(SEQ, MODEL),
            out(SEQ, MODEL),
            out(FFN, SEQ),
            out(FFN, SEQ),
            out(FFN, SEQ),
            out(2, SEQ, BLOCK),
            out(2, SEQ, BLOCK),
        ),
        scratch_shapes=[pltpu.VMEM((FFN, MODEL), BF16)] * 3 + [pltpu.SemaphoreType.DMA((48,))],
        compiler_params=params(),
    )(table, where, *h, *cot, gains, *blocks)


def down_kernel(table, where, act_a, act_b, *refs):
    blocks, (keep_a, send_a, keep_b, send_b, w, sems) = refs[:5], refs[5:]
    wait(fetch(table, blocks, w, sems, 2 * FFN))
    put_chunks(tn(act_a[...], w[...]), where, keep_a, send_a)
    for k in range(2):
        value = tn(act_b[...], w[:, 2 * k * BLOCK : (2 * k + 2) * BLOCK])
        keep_b[k] = narrow(value[:, :BLOCK])
        send_b[k] = narrow(value[:, BLOCK:])


def down(table, where, act_a, act_b, blocks):
    chunk = spec((2, SEQ, BLOCK))
    return pl.pallas_call(
        down_kernel,
        in_specs=[SCALARS] * 2 + whole(act_a, act_b) + [ANYWHERE] * 5,
        out_specs=(chunk,) * 4,
        out_shape=(out(2, SEQ, BLOCK),) * 4,
        scratch_shapes=[pltpu.VMEM((FFN, MODEL), BF16), pltpu.SemaphoreType.DMA((16,))],
        compiler_params=params(),
    )(table, where, act_a, act_b, *blocks)


ORDER = (8, 9, 10, 11, 4, 5, 6, 7, 12, 13, 14, 15, 0, 1, 2, 3)


def two_pieces(table, ref):
    step = pl.program_id(0)
    starts = [pl.multiple_of(table[2 * step + k], 128) for k in range(2)]
    return jnp.concatenate([ref[:, pl.ds(start, 128)] for start in starts], 1)


def put_pieces(refs, parts):
    step = pl.program_id(0)
    for ref, first, last in zip(refs, (0, 1, 2, 4, 6), (0, 1, 3, 5, 7), strict=True):

        @pl.when((step >= first) & (step <= last))
        def _(ref=ref):
            for at, value in parts:
                for k in range(2):
                    ref[k, at : at + value.shape[0]] = narrow(value[:, k * 128 : (k + 1) * 128])


def pieces_specs(rows):
    specs, shapes = [], []
    for first, count in zip((0, 1, 2, 4, 6), (1, 1, 2, 2, 2), strict=True):
        specs.append(
            spec((2, rows, 128), lambda s, f=first, c=count: (jnp.clip(s - f, 0, c - 1), 0, 0))
        )
        shapes.append(out(2 * count, rows, 128))
    return tuple(specs), tuple(shapes)


def grads_mlp_kernel(table, dg_a, du_a, act_a, n_a, cot_a, dg_b, du_b, act_b, n_b, cot_b, *outs):
    n0, n1 = two_pieces(table, n_a), two_pieces(table, n_b)
    c0, c1 = two_pieces(table, cot_a), two_pieces(table, cot_b)
    parts = [
        (0, nn(dg_a[...], n0) + nn(dg_b[...], n1)),
        (FFN, nn(du_a[...], n0) + nn(du_b[...], n1)),
        (2 * FFN, nn(act_a[...], c0) + nn(act_b[...], c1)),
    ]
    put_pieces(outs, parts)


def grads_mlp(table, a, b):
    specs, shapes = pieces_specs(3 * FFN)
    return pl.pallas_call(
        grads_mlp_kernel,
        grid=(8,),
        in_specs=[SCALARS] + whole(*a, *b),
        out_specs=specs,
        out_shape=shapes,
        compiler_params=params(),
    )(table, *a, *b)


def residual_kernel(table, a0, a1, a2, a3, h, r, cot, gains, *refs):
    blocks, (e_o, dh_o, do_o, gain_o, w, sems) = refs[:5], refs[5:]

    @pl.when(pl.program_id(0) == 0)
    def _():
        gain_o[...] = jnp.zeros_like(gain_o)
        wait(fetch(table, blocks, w, sems, QKV))

    raw = wide(jnp.concatenate([a0[...], a1[...], a2[...], a3[...]], 1))
    scale = r[...]
    unit = wide(h[...]) * scale
    gain_o[...] += jnp.sum(raw * unit, 0, keepdims=True)
    a = raw * wide(gains[1:2, :])
    d_h = wide(cot[...]) + scale * (a - unit * jnp.mean(a * unit, -1, keepdims=True))
    dh_o[...] = d_h[:, :BLOCK]
    e = narrow(d_h)
    e_o[...] = e
    do_o[...] = narrow(nt(w[...], e))


def residual(table, a, h, r, cot, gains, blocks):
    t = 256
    row = lambda i: (i, 0)
    return pl.pallas_call(
        residual_kernel,
        grid=(SEQ // t,),
        in_specs=[SCALARS]
        + [spec((t, BLOCK), row)] * 4
        + [spec((t, MODEL), row), spec((t, 1), row), spec((t, MODEL), row)]
        + whole(gains)
        + [ANYWHERE] * 5,
        out_specs=(
            spec((t, MODEL), row),
            spec((t, BLOCK), row),
            spec((QROWS, t), lambda i: (0, i)),
            spec((1, MODEL)),
        ),
        out_shape=(
            out(SEQ, MODEL),
            out(SEQ, BLOCK, dtype=F32),
            out(QROWS, SEQ),
            out(1, MODEL, dtype=F32),
        ),
        scratch_shapes=[pltpu.VMEM((QROWS, MODEL), BF16), pltpu.SemaphoreType.DMA((16,))],
        compiler_params=params(),
    )(table, *a, h, r, cot, gains, *blocks)


def attend_back_kernel(q, do, p, k, v, cos, sin, dq_o, dkv_o, dk, dv):
    h = pl.program_id(0)

    @pl.when(h == 0)
    def _():
        dk[...] = jnp.zeros_like(dk)
        dv[...] = jnp.zeros_like(dv)

    c, s = cos[...], sin[...]
    scale = 1.0 / math.sqrt(HEAD)
    low = p[0]
    probs = wide(low)
    dp = tn(v[...], do[...])
    ds = narrow(probs * (dp - jnp.sum(probs * dp, 0, keepdims=True)))
    dq_o[...] = narrow(rotated_back(nn(k[...], ds) * scale, c, s))
    dk[...] += nt(q[...], ds)
    dv[...] += nt(do[...], low)

    @pl.when(h == pl.num_programs(0) - 1)
    def _():
        dkv_o[:HEAD, :] = narrow(rotated_back(dk[...] * scale, c, s))
        dkv_o[HEAD:, :] = narrow(dv[...])


def attend_back(q, do, p, k, v, cos, sin):
    heads = QROWS // HEAD
    head = lambda h: (h, 0)
    return pl.pallas_call(
        attend_back_kernel,
        grid=(heads,),
        in_specs=[spec((HEAD, SEQ), head)] * 2
        + [spec((1, SEQ, SEQ), lambda h: (h, 0, 0))]
        + whole(k, v, cos, sin),
        out_specs=(spec((HEAD, SEQ), head), spec((2 * HEAD, SEQ))),
        out_shape=(out(QROWS, SEQ), out(2 * HEAD, SEQ)),
        scratch_shapes=[pltpu.VMEM((HEAD, SEQ), F32)] * 2,
        compiler_params=params(),
    )(q, do, p, k, v, cos, sin)


def input_back_kernel(table, dq, dkv, x, r, gains, *refs):
    blocks, (keep_o, send_o, stat_o, gain_o, w, sems) = refs[:5], refs[5:]

    @pl.when(pl.program_id(0) == 0)
    def _():
        gain_o[...] = jnp.zeros_like(gain_o)
        wait(fetch(table, blocks, w, sems, 0))

    part = tn(dq[...], w[:QROWS, :]) + tn(dkv[...], w[QROWS:, :])
    unit = wide(x[...]) * r[...]
    product = part * unit
    gain_o[...] += jnp.sum(product, 0, keepdims=True)
    stat_o[...] = jnp.sum(product * wide(gains[0:1, :]), -1, keepdims=True)
    for k in range(2):
        keep_o[k] = narrow(part[:, 2 * k * BLOCK : (2 * k + 1) * BLOCK])
        send_o[k] = narrow(part[:, (2 * k + 1) * BLOCK : (2 * k + 2) * BLOCK])


def input_back(table, dq, dkv, x, r, gains, blocks):
    t = 256
    row = lambda i: (i, 0)
    chunk = spec((2, t, BLOCK), lambda i: (0, i, 0))
    return pl.pallas_call(
        input_back_kernel,
        grid=(SEQ // t,),
        in_specs=[SCALARS]
        + [spec((QROWS, t), lambda i: (0, i)), spec((2 * HEAD, t), lambda i: (0, i))]
        + [spec((t, MODEL), row), spec((t, 1), row)]
        + whole(gains)
        + [ANYWHERE] * 5,
        out_specs=(chunk, chunk, spec((t, 1), row), spec((1, MODEL))),
        out_shape=(
            out(2, SEQ, BLOCK),
            out(2, SEQ, BLOCK),
            out(SEQ, 1, dtype=F32),
            out(1, MODEL, dtype=F32),
        ),
        scratch_shapes=[pltpu.VMEM((QKV, MODEL), BF16), pltpu.SemaphoreType.DMA((16,))],
        compiler_params=params(),
    )(table, dq, dkv, x, r, gains, *blocks)


def grads_attention_kernel(table, dq, dkv, o, n, e, gain, *outs):
    n_part, e_part = two_pieces(table, n), two_pieces(table, e)
    parts = [
        (0, nn(dq[...], n_part)),
        (QROWS, nn(dkv[...], n_part)),
        (QKV, nn(o[...], e_part)),
        (GAINS_AT, two_pieces(table, gain)),
    ]
    put_pieces(outs, parts)


def grads_attention(table, *arrays):
    specs, shapes = pieces_specs(GAINS_AT + GAINS)
    return pl.pallas_call(
        grads_attention_kernel,
        grid=(8,),
        in_specs=[SCALARS] + whole(*arrays),
        out_specs=specs,
        out_shape=shapes,
        compiler_params=params(),
    )(table, *arrays)


def outputs_kernel(h, m, dh, c, x, r, stat, gains, mixed_o, grad_o):
    mixed_o[...] = narrow(to_natural(h[...] + m[...]))
    unit = wide(x[...]) * r[...]
    c_full = c[...] * wide(gains[0:1, :])
    grad_o[...] = to_natural(dh[...] + r[...] * (c_full - unit * (stat[...] * (1.0 / MODEL))))


def outputs(h, m, dh, c, x, r, stat, gains):
    t = 256
    row = lambda i: (i, 0)
    part = spec((t, BLOCK), row)
    one = spec((t, 1), row)
    return pl.pallas_call(
        outputs_kernel,
        grid=(SEQ // t,),
        in_specs=[part, part, part, part, part, one, one, spec((GAINS, BLOCK))],
        out_specs=(part, part),
        out_shape=(out(SEQ, BLOCK), out(SEQ, BLOCK, dtype=F32)),
        compiler_params=params(),
    )(h, m, dh, c, x, r, stat, gains)


def sum_eight(keep_self, send_self, keep_other, send_other):
    first, second = cross(False), cross(True)
    other = narrow(wide(keep_other) + wide(swap_core(send_other)))
    own = narrow(wide(keep_self) + wide(swap_core(send_self)))
    through = first(own[1])
    return (
        wide(own[0])
        + wide(first(other[0]))
        + wide(second(narrow(wide(other[1]) + wide(through))))
    )


def sum_four(keep, send):
    s = narrow(wide(keep) + wide(swap_core(send)))
    return wide(s[0]) + wide(swap_xh(s[1]))


def gather_four(v):
    other = swap_xh(v)
    return v, swap_core(v), other, swap_core(other)


def gather_eight(v):
    first, second = cross(False), cross(True)
    a, b = first(v), second(v)
    opposite = second(a)
    own = (v, swap_core(v), opposite, swap_core(opposite))
    return own, (a, swap_core(a), b, swap_core(b))


def shards(
    tokens,
    w_query,
    key_value_weight,
    w_output,
    w_gate,
    w_up,
    w_down,
    gain_attention,
    gain_mlp,
    segment,
    position,
    cotangent,
):
    core = lax.axis_index("core")
    col = lax.axis_index("xh") * 2 + core
    upper = lax.axis_index("xl") == 1
    far, close = jnp.arange(4)[:, None], jnp.arange(4)[None, :]
    y = (lax.axis_index("y") ^ col) ^ jnp.where(core == 0, far, close)
    z = lax.axis_index("z") ^ jnp.where(core == 0, close, far)
    table = ((y * 4 + z) * 128).reshape(16).astype(jnp.int32)
    order = table[jnp.array(ORDER)]
    self_at = jnp.array([0, BLOCK, 2 * BLOCK, 3 * BLOCK, 0, 0], jnp.int32)
    other_at = jnp.stack(
        [
            2 * BLOCK * core,
            BLOCK + 2 * BLOCK * (1 - core),
            2 * BLOCK * (1 - core),
            BLOCK + 2 * BLOCK * core,
            core,
            1 - core,
        ]
    ).astype(jnp.int32)

    gains_in = jnp.concatenate(
        [gain_attention[:, None], gain_mlp[:, None], jnp.zeros((64, GAINS - 2), BF16)], 1
    )
    attn_rows = jnp.concatenate([w_query, key_value_weight, w_output.T, gains_in], 1)
    attn_other = swap_xl(attn_rows)
    attn_shard = jnp.where(
        upper,
        jnp.concatenate([attn_other, attn_rows], 0),
        jnp.concatenate([attn_rows, attn_other], 0),
    ).T
    attn_blocks = gather_two(attn_shard)

    def halves(v):
        return jnp.where(upper, v[FFN:], v[:FFN]), jnp.where(upper, v[:FFN], v[FFN:])

    (g_keep, g_send), (u_keep, u_send), (d_keep, d_send) = (
        halves(w_gate.T),
        halves(w_up.T),
        halves(w_down),
    )
    mlp_keep = jnp.concatenate([g_keep, u_keep, d_keep], 0)
    mlp_send = jnp.concatenate([g_send, u_send, d_send], 0)
    cut = 3 * FFN // 2
    mlp_sent = swap_xl(jnp.concatenate([mlp_send[:cut], mlp_send[cut:]], 1))
    mlp_other = jnp.concatenate([mlp_sent[:, :64], mlp_sent[:, 64:]], 0)
    mlp_shard = jnp.where(
        upper,
        jnp.concatenate([mlp_other, mlp_keep], 1),
        jnp.concatenate([mlp_keep, mlp_other], 1),
    )
    mlp_blocks = gather_two(mlp_shard)

    frequency = jnp.exp(jnp.arange(HALF).astype(F32) * (-2.0 * math.log(10000.0) / HEAD))
    angles = frequency[:, None] * position.astype(F32)[None, :]
    cos, sin = jnp.cos(angles), jnp.sin(angles)
    x_own, cot_own = to_inner(tokens, cotangent)
    x_full, normed_one, r_one, q, k, v, gains = project(
        table, gather_four(x_own), attn_blocks, cos, sin
    )
    o, probs = attend(q, k, v, segment[None, :], segment[:, None])
    resid = wide(x_own) + sum_four(*out_project(table, o, attn_blocks))
    h_self, h_other = gather_eight(narrow(resid))
    cot_self, cot_other = gather_eight(cot_own)
    n_a, _, _, cot_a, act_a, dg_a, du_a, keep_other, send_other = mlp(
        table, other_at, h_other, cot_other, gains, mlp_blocks
    )
    n_b, r_two, h_full, cot_b, act_b, dg_b, du_b, keep_self, send_self = mlp(
        table, self_at, h_self, cot_self, gains, mlp_blocks
    )
    d_normed_two = narrow(sum_eight(keep_self, send_self, keep_other, send_other))
    mlp_terms = grads_mlp(
        order, (dg_a, du_a, act_a, n_a, cot_a), (dg_b, du_b, act_b, n_b, cot_b)
    )
    keep_other, send_other, keep_self, send_self = down(table, other_at, act_a, act_b, mlp_blocks)
    mlp_out = sum_eight(keep_self, send_self, keep_other, send_other)
    e, d_resid, d_o, gain_two = residual(
        table, gather_four(d_normed_two), h_full, r_two, cot_b, gains, attn_blocks
    )
    d_q, d_kv = attend_back(q, d_o, probs, k, v, cos, sin)
    keep, send, stat, gain_one = input_back(table, d_q, d_kv, x_full, r_one, gains, attn_blocks)
    d_normed_one = sum_four(keep, send)
    stat = stat.reshape(4, 128)
    stat = stat + swap_core(stat)
    stat = (stat + swap_xh(stat)).reshape(SEQ, 1)
    mixed, input_grad = outputs(
        resid, mlp_out, d_resid, d_normed_one, x_full, r_one, stat, gains
    )

    gain_rows = jnp.concatenate([gain_one, gain_two, jnp.zeros((GAINS - 2, MODEL), F32)], 0)
    attn_terms = grads_attention(order, d_q, d_kv, o, normed_one, e, gain_rows)

    def lanes(value):
        return jnp.where(upper, value[:, 64:], value[:, :64]), jnp.where(
            upper, value[:, :64], value[:, 64:]
        )

    mlp_mine, mlp_theirs = lanes(reduce_two(mlp_terms))
    mlp_theirs = wide(swap_xl(narrow(mlp_theirs)))

    def joined(k):
        mine, theirs = mlp_mine[k * FFN : (k + 1) * FFN], mlp_theirs[k * FFN : (k + 1) * FFN]
        return jnp.where(
            upper, jnp.concatenate([theirs, mine], 0), jnp.concatenate([mine, theirs], 0)
        )

    grad_gate, grad_up, grad_down = joined(0).T, joined(1).T, joined(2)
    attn_sum = reduce_two(attn_terms)
    attn_mine, attn_theirs = lanes(attn_sum)
    attn_mine = attn_mine + wide(swap_xl(narrow(attn_theirs)))
    grad_query = attn_mine[:QROWS].T
    grad_keyval = attn_mine[QROWS:QKV].T
    grad_output = attn_mine[QKV:GAINS_AT]
    gain_one = attn_mine[GAINS_AT]
    gain_one = gain_one + swap_core(gain_one)
    gain_one = gain_one + swap_xh(gain_one)
    gain_two = attn_mine[GAINS_AT + 1]
    return (
        mixed,
        input_grad,
        grad_query,
        grad_keyval,
        grad_output,
        grad_gate,
        grad_up,
        grad_down,
        gain_one,
        gain_two,
    )


def solution(mesh):
    fine = Mesh(mesh.devices.reshape(SIZES), AXES)
    both, turned, rows = P(ROW, COL), P(COL, ROW), P(ROW)
    return jax.shard_map(
        shards,
        mesh=fine,
        in_specs=(both, both, both, turned, both, both, turned, rows, rows, rows, rows, both),
        out_specs=(both, both, both, both, turned, both, both, turned, rows, rows),
        check_vma=False,
    )
```

```python
import functools
import math

import jax
import jax.numpy as jnp
from jax import lax
from jax.experimental import pallas as pl
from jax.experimental.pallas import tpu as pltpu
from jax.sharding import Mesh, PartitionSpec as P

F32, BF16 = jnp.float32, jnp.bfloat16
HEAD = 64
HALF = HEAD // 2
SCALE = 1.0 / math.sqrt(HEAD)
EPSILON = 1e-05
MASKED = -1e30
AXES = ("y", "xl", "z", "xh", "core")
SIZES = (4, 2, 4, 2, 2)
ROW, COL = ("y", "xl", "z"), ("xh", "core")

SEQ = 512
QUERIES = 256
TOGETHER = 4
MODEL = 2048
BLOCK = 512
QROWS = 512
QKV = QROWS + 128
GAINS_AT = QKV + 512
GAINS = 32
FFN = 704


def turn(second, mask):
    pairs = []
    for i in range(32):
        shift = 1 if (i % 2 == 0) != second else 3
        pairs.append((i, i ^ (mask << shift)))
    return lambda v: lax.ppermute(v, ("y", "z", "core"), pairs)


def cross(second):
    pairs = []
    for i in range(8):
        near = (i % 2 == 0) != second
        pairs.append((i, i ^ (4 if near else 6)))
    return lambda v: lax.ppermute(v, ("xl", "xh", "core"), pairs)


def swap_core(v):
    return lax.ppermute(v, "core", [(0, 1), (1, 0)])


def swap_xh(v):
    return lax.ppermute(v, "xh", [(0, 1), (1, 0)])


def swap_both(v):
    return lax.ppermute(v, ("xh", "core"), [(i, i ^ 3) for i in range(4)])


def swap_xl(v):
    return lax.ppermute(v, "xl", [(0, 1), (1, 0)])


def narrow(v):
    return v.astype(BF16)


def wide(v):
    return v.astype(F32)


def gather_two(v, after):
    held = bundle([v] + [turn(False, mask)(v) for mask in (1, 2, 3)], after)
    near, far = turn(True, 1), turn(True, 3)
    from_near, from_far = near(held), far(held)
    first, last = halves(from_near, from_far)
    return held, from_near, far(first), near(last), from_far


def reduce_start(terms, after):
    low, high, one, three, own = terms
    return (*add_halves(one, three, turn(True, 1)(low), turn(True, 3)(high), after), own)


def reduce_end(one, three, own, after):
    parts = sum_blocks(own, turn(True, 1)(one), turn(True, 3)(three), after)
    return [parts[0]] + [turn(False, mask)(parts[mask]) for mask in (1, 2, 3)]


def dot(a, b, contract):
    return lax.dot_general(a, b, ((contract[:1], contract[1:]), ((), ())), preferred_element_type=F32)


def nn(a, b):
    return dot(a, b, (1, 0))


def nt(a, b):
    return dot(a, b, (1, 1))


def tn(a, b):
    return dot(a, b, (0, 0))


def params(mib=14):
    return pltpu.CompilerParams(vmem_limit_bytes=mib * 1024 * 1024)


def cost(us):
    return pl.CostEstimate(flops=int(us * 1.15e9), bytes_accessed=0, transcendentals=0)


def spec(shape, index=None):
    zeros = (0,) * len(shape)
    return pl.BlockSpec(shape, index if index is not None else (lambda *_: zeros))


def whole(*arrays):
    return [spec(a.shape) for a in arrays]


def out(*shape, dtype=BF16):
    return jax.ShapeDtypeStruct(shape, dtype)


def lane_low(shape):
    return lax.broadcasted_iota(jnp.int32, shape, 1) < 64


def pair(a, b):
    low = lane_low(a.shape)
    return jnp.where(low, a, pltpu.roll(b, 64, 1)), jnp.where(low, pltpu.roll(a, 64, 1), b)


def tie_kernel(*refs):
    pass


def tie(arrays, *after):
    count = len(arrays)
    return pl.pallas_call(
        tie_kernel,
        in_specs=[ANYWHERE] * (count + len(after)),
        out_specs=(ANYWHERE,) * count,
        out_shape=tuple(jax.ShapeDtypeStruct(v.shape, v.dtype) for v in arrays),
        input_output_aliases={k: k for k in range(count)},
        compiler_params=params(),
        cost_estimate=cost(1),
    )(*arrays, *after)


def inner(src, dst):
    t = [wide(src[:, k * 128 : (k + 1) * 128]) for k in range(4)]
    z0, z1 = pair(t[0], t[2])
    z2, z3 = pair(t[1], t[3])
    for k, value in enumerate((z0, z1, z2, z3)):
        dst[:, k * 128 : (k + 1) * 128] = narrow(value)


def column(row):
    n = row.shape[1]
    here = lax.broadcasted_iota(jnp.int32, (n, n), 0) == lax.broadcasted_iota(jnp.int32, (n, n), 1)
    return jnp.sum(jnp.where(here, wide(row[...]), 0.0), 1, keepdims=True)


def prepare_kernel(tokens, cot, w_q, w_kv, w_o, gain_a, gain_m, x_o, cot_o, rows_o):
    rows_o[:, :QROWS] = w_q[...]
    rows_o[:, QROWS:QKV] = w_kv[...]
    rows_o[:, QKV:GAINS_AT] = w_o[...]
    lane = lax.broadcasted_iota(jnp.int32, (64, GAINS), 1)
    gains = jnp.where(lane == 0, column(gain_a), jnp.where(lane == 1, column(gain_m), 0.0))
    rows_o[:, GAINS_AT:] = narrow(gains)
    inner(tokens, x_o)
    inner(cot, cot_o)


def prepare(tokens, cot, w_q, w_kv, w_o, gain_a, gain_m):
    shapes = (out(*tokens.shape), out(*cot.shape), out(64, GAINS_AT + GAINS))
    args = (tokens, cot, w_q, w_kv, w_o, gain_a[None, :], gain_m[None, :])
    return pl.pallas_call(
        prepare_kernel,
        in_specs=whole(*args),
        out_specs=tuple(whole(*shapes)),
        out_shape=shapes,
        compiler_params=params(),
        cost_estimate=cost(3),
    )(*args)


def shard_attention_kernel(where, mine, other, *refs):
    upper = where[6] == 1
    a, b = wide(mine[...]), wide(other[...])
    rows = jnp.concatenate([jnp.where(upper, b, a), jnp.where(upper, a, b)], 0)
    refs[-1][...] = narrow(rows.T)


def shard_attention(where, mine, other, after):
    shape = out(mine.shape[1], 128)
    return pl.pallas_call(
        shard_attention_kernel,
        in_specs=[SCALARS] + whole(mine, other) + [ANYWHERE] * len(after),
        out_specs=spec(shape.shape),
        out_shape=shape,
        compiler_params=params(),
        cost_estimate=cost(2),
    )(where, mine, other, *after)


def prepare_mlp_kernel(where, w_g, w_u, w_d, keep_o, pack_o, held):
    for k, w in enumerate((w_g, w_u, w_d)):
        value = wide(w[...])
        both = jnp.concatenate([value[:, :FFN], value[:, FFN:]], 0)
        held[k * FFN : (k + 1) * FFN] = both.T
    keep_o[...] = narrow(held[...])
    pack_o[...] = narrow(packed(held[...], where[6] == 1))


def prepare_mlp(where, w_g, w_u, w_d):
    rows = 3 * FFN
    shapes = (out(rows, 128), out(rows // 2, 128))
    return pl.pallas_call(
        prepare_mlp_kernel,
        in_specs=[SCALARS] + whole(w_g, w_u, w_d),
        out_specs=tuple(whole(*shapes)),
        out_shape=shapes,
        scratch_shapes=[pltpu.VMEM((rows, 128), F32)],
        compiler_params=params(),
        cost_estimate=cost(4),
    )(where, w_g, w_u, w_d)


def sum_terms_kernel(a, b, c, d, total_o):
    total_o[...] = narrow(wide(a[...]) + wide(b[...]) + wide(c[...]) + wide(d[...]))


def sum_terms(terms):
    shape = out(*terms[0].shape)
    return pl.pallas_call(
        sum_terms_kernel,
        in_specs=whole(*terms),
        out_specs=spec(shape.shape),
        out_shape=shape,
        compiler_params=params(),
        cost_estimate=cost(2),
    )(*terms)


def add_split_kernel(a, b, *outs):
    for k, ref in enumerate(outs):
        ref[...] = narrow(wide(a[k]) + wide(b[k]))


def add_cores(keep, send):
    shapes = (out(*keep.shape[1:]),) * keep.shape[0]
    return pl.pallas_call(
        add_split_kernel,
        in_specs=whole(keep, send),
        out_specs=tuple(whole(*shapes)),
        out_shape=shapes,
        compiler_params=params(),
        cost_estimate=cost(2),
    )(keep, swap_core(send))


def to_natural(v):
    z = [v[:, k * 128 : (k + 1) * 128] for k in range(4)]
    t0, t2 = pair(z[0], z[1])
    t1, t3 = pair(z[2], z[3])
    return jnp.concatenate([t0, t1, t2, t3], 1)


def fetch(table, blocks, target, sems, start):
    rows = target.shape[0]
    copies = []
    for j in range(4):
        for i in range(4):
            src = block_of(blocks, j, i)
            lanes = pl.multiple_of(table[4 * j + i], 128)
            copy = pltpu.make_async_copy(
                src.at[pl.ds(start, rows)], target.at[:, pl.ds(lanes, 128)], sems.at[len(copies)]
            )
            copy.start()
            copies.append(copy)
    return copies


def block_of(blocks, j, i):
    own, one, low, high, three = blocks
    if j == 2:
        return low.at[i] if i < 2 else high.at[i - 2]
    return (own, one, None, three)[j].at[i]


def wait(copies):
    for copy in copies:
        copy.wait()


ANYWHERE = pl.BlockSpec(memory_space=pl.ANY)
SCALARS = pl.BlockSpec(memory_space=pltpu.SMEM)


def halves_kernel(a, b, a_o, b_o):
    a_o[...] = a[...]
    b_o[...] = b[...]


def halves(a, b):
    block = (2,) + a.shape[1:]
    first = spec(block, lambda i: (0, 0, 0))
    return pl.pallas_call(
        halves_kernel,
        grid=(1,),
        in_specs=[first, spec(block, lambda i: (1, 0, 0))],
        out_specs=(first, first),
        out_shape=(out(*block),) * 2,
        compiler_params=params(),
        cost_estimate=cost(2),
    )(a, b)


def add_halves_kernel(one, three, low, high, *refs):
    one_o, three_o = refs[-2:]
    three_o[...] = narrow(wide(three[...]) + wide(low[...]))
    one_o[...] = narrow(wide(one[...]) + wide(high[...]))


def add_halves(one, three, low, high, after):
    block = (1,) + one.shape[1:]
    first, last = spec(block, lambda i: (i, 0, 0)), spec(block, lambda i: (2 + i, 0, 0))
    return pl.pallas_call(
        add_halves_kernel,
        grid=(2,),
        in_specs=[last, first, first, first] + [ANYWHERE] * len(after),
        out_specs=(last, first),
        out_shape=(out(*one.shape),) * 2,
        input_output_aliases={0: 0, 1: 1},
        compiler_params=params(),
        cost_estimate=cost(2),
    )(one, three, low, high, *after)


def sum_blocks_kernel(a, b, c, *refs):
    for k, ref in enumerate(refs[-4:]):
        ref[...] = narrow(wide(a[k]) + wide(b[k]) + wide(c[k]))


def sum_blocks(a, b, c, after):
    shapes = (out(*a.shape[1:]),) * 4
    return pl.pallas_call(
        sum_blocks_kernel,
        in_specs=whole(a, b, c) + [ANYWHERE] * len(after),
        out_specs=tuple(whole(*shapes)),
        out_shape=shapes,
        compiler_params=params(),
        cost_estimate=cost(3),
    )(a, b, c, *after)


def packed(v, upper):
    half = v.shape[0] // 2
    top, bottom = v[:half], v[half:]
    low = lane_low(top.shape)
    return jnp.where(
        upper,
        jnp.where(low, top, pltpu.roll(bottom, 64, 1)),
        jnp.where(low, pltpu.roll(top, 64, 1), bottom),
    )


def unpacked(v, upper):
    turned = pltpu.roll(v, 64, 1)
    return [jnp.where(upper, v, turned), jnp.where(upper, turned, v)]


def own_lanes(shape, upper):
    return lane_low(shape) != upper


def sum_pack_kernel(where, *refs, count):
    sum_o, pack_o = refs[-2:]
    total = wide(refs[0][...])
    for ref in refs[1:count]:
        total += wide(ref[...])
    sum_o[...] = total
    pack_o[...] = narrow(packed(total, where[6] == 1))


def sum_pack(where, parts, after):
    rows = parts[0].shape[0]
    shapes = (out(rows, 128, dtype=F32), out(rows // 2, 128))
    return pl.pallas_call(
        functools.partial(sum_pack_kernel, count=len(parts)),
        in_specs=[SCALARS] + whole(*parts) + [ANYWHERE] * len(after),
        out_specs=tuple(whole(*shapes)),
        out_shape=shapes,
        compiler_params=params(),
        cost_estimate=cost(2),
    )(where, *parts, *after)


def merge_kernel(where, keep, other, *refs):
    upper = where[6] == 1
    half = other.shape[0]
    for k, part in enumerate(unpacked(wide(other[...]), upper)):
        rows = slice(k * half, (k + 1) * half)
        refs[-1][rows] = narrow(
            jnp.where(own_lanes(part.shape, upper), wide(keep[rows, :]), part)
        )


def merge(where, keep, other, after):
    return pl.pallas_call(
        merge_kernel,
        in_specs=[SCALARS] + whole(keep, other) + [ANYWHERE] * len(after),
        out_specs=spec(keep.shape),
        out_shape=out(*keep.shape),
        compiler_params=params(),
        cost_estimate=cost(2),
    )(where, keep, other, *after)


def row_dot(weight, grad):
    return jnp.sum(wide(weight) * grad, -1, keepdims=True)


def finish_mlp_kernel(where, total, other, w_gate, w_up, gate_o, up_o, down_o, sum_o, held):
    upper = where[6] == 1
    half = other.shape[0]
    for k, part in enumerate(unpacked(wide(other[...]), upper)):
        rows = slice(k * half, (k + 1) * half)
        held[rows] = jnp.where(own_lanes(part.shape, upper), total[rows, :], part)
    for k, ref in enumerate((gate_o, up_o, down_o)):
        turned = held[k * FFN : (k + 1) * FFN].T
        ref[:, :FFN] = turned[:64]
        ref[:, FFN:] = turned[64:]
    sum_o[...] = row_dot(w_gate[...], gate_o[...]) + row_dot(w_up[...], up_o[...])


def finish_mlp(where, total, other, w_gate, w_up):
    shapes = (out(64, 2 * FFN, dtype=F32),) * 3 + (out(64, 1, dtype=F32),)
    return pl.pallas_call(
        finish_mlp_kernel,
        in_specs=[SCALARS] + whole(total, other, w_gate, w_up),
        out_specs=tuple(whole(*shapes)),
        out_shape=shapes,
        scratch_shapes=[pltpu.VMEM(total.shape, F32)],
        compiler_params=params(),
        cost_estimate=cost(4),
    )(where, total, other, w_gate, w_up)


def finish_attention_kernel(where, total, other, w_q, w_kv, q_o, kv_o, out_o, sum_o, held):
    upper = where[6] == 1
    half = other.shape[0]
    for k, part in enumerate(unpacked(wide(other[...]), upper)):
        rows = slice(k * half, (k + 1) * half)
        held[:, rows] = (total[rows, :] + pltpu.roll(part, 64, 1)).T
    mine = held[pl.ds(pl.multiple_of(where[6] * 64, 64), 64), :]
    q_o[...] = mine[:, :QROWS]
    kv_o[...] = mine[:, QROWS:QKV]
    out_o[...] = mine[:, QKV:]
    sum_o[...] = row_dot(w_q[...], q_o[...]) + row_dot(w_kv[...], kv_o[...])


def finish_attention(where, total, other, w_q, w_kv):
    shapes = tuple(out(64, n, dtype=F32) for n in (QROWS, QKV - QROWS, QROWS, 1))
    return pl.pallas_call(
        finish_attention_kernel,
        in_specs=[SCALARS] + whole(total, other, w_q, w_kv),
        out_specs=tuple(whole(*shapes)),
        out_shape=shapes,
        scratch_shapes=[pltpu.VMEM((128, total.shape[0]), F32)],
        compiler_params=params(),
        cost_estimate=cost(3),
    )(where, total, other, w_q, w_kv)


def rotated(v, cos, sin):
    a, b = v[:HALF], v[HALF:]
    return jnp.concatenate([a * cos - b * sin, b * cos + a * sin], 0)


def rotated_back(v, cos, sin):
    a, b = v[:HALF], v[HALF:]
    return jnp.concatenate([a * cos + b * sin, b * cos - a * sin], 0)


def bundle_kernel(*refs):
    for k in range(4):
        refs[-1][k] = refs[k][...]


def bundle(parts, after):
    shape = out(4, *parts[0].shape)
    return pl.pallas_call(
        bundle_kernel,
        in_specs=whole(*parts) + [ANYWHERE] * len(after),
        out_specs=spec(shape.shape),
        out_shape=shape,
        compiler_params=params(),
        cost_estimate=cost(2),
    )(*parts, *after)


def attention_kernel(table, x0, x1, x2, x3, cos, sin, segment, *refs):
    blocks, refs = refs[:5], refs[-20:]
    n_o, p_o, r_o, q_o, k_o, v_o, gains_o, o_o, keep_o, send_o = refs[:10]
    w, w_out, n, probs, bias, w_sems, out_sems, gain_sems, n_sem, p_sems = refs[10:]
    copies = fetch(table, blocks, gains_o, gain_sems, GAINS_AT)
    w_copies = fetch(table, blocks, w, w_sems, 0)
    out_copies = fetch(table, blocks, w_out, out_sems, QKV)
    x = wide(jnp.concatenate([x0[...], x1[...], x2[...], x3[...]], 1))
    r = lax.rsqrt(jnp.mean(x * x, -1, keepdims=True) + EPSILON)
    r_o[...] = r
    wait(copies)
    n[...] = narrow(x * r * wide(gains_o[0:1, :]))
    saved = [pltpu.make_async_copy(n, n_o, n_sem)]
    saved[0].start()

    shape = (SEQ, SEQ)
    key = lax.broadcasted_iota(jnp.int32, shape, 0)
    query = lax.broadcasted_iota(jnp.int32, shape, 1)
    allowed = (column(segment) == wide(segment[...])) & (key <= query)
    bias[...] = jnp.where(allowed, 0.0, MASKED)

    wait(w_copies)
    qkv = nt(w[...], n[...])
    c, s = cos[...], sin[...]
    for h in range(QROWS // HEAD):
        head = rotated(qkv[h * HEAD : (h + 1) * HEAD], c, s)
        q_o[h * HEAD : (h + 1) * HEAD, :] = narrow(head) * SCALE
    k_o[...] = narrow(rotated(qkv[QROWS : QROWS + HEAD], c, s))
    v_o[...] = narrow(qkv[QROWS + HEAD :])

    for first in range(0, QROWS // HEAD, TOGETHER):
        for start in range(0, SEQ, QUERIES):
            stop = start + QUERIES
            queries = slice(start, stop)
            for h in range(first, first + TOGETHER):
                rows = slice(h * HEAD, (h + 1) * HEAD)
                s = tn(k_o[:, :stop], q_o[rows, queries]) + bias[:stop, queries]
                e = jnp.exp(s - jnp.max(s, 0, keepdims=True))
                probs[h, :stop, queries] = narrow(e * (1.0 / jnp.sum(e, 0, keepdims=True)))
            for h in range(first, first + TOGETHER):
                rows = slice(h * HEAD, (h + 1) * HEAD)
                o_o[rows, queries] = narrow(nn(v_o[:, :stop], probs[h, :stop, queries]))
        some = pl.ds(first, TOGETHER)
        saved.append(pltpu.make_async_copy(probs.at[some], p_o.at[some], p_sems.at[first]))
        saved[-1].start()

    wait(out_copies)
    value = tn(o_o[...], w_out[...])
    for k in range(4):
        (keep_o, send_o)[k % 2][k // 2] = narrow(value[:, k * BLOCK : (k + 1) * BLOCK])
    wait(saved)


def attention(table, x, cos, sin, segment, blocks):
    heads = QROWS // HEAD
    shapes = (
        out(SEQ, 1, dtype=F32),
        out(QROWS, SEQ),
        out(HEAD, SEQ),
        out(HEAD, SEQ),
        out(GAINS, MODEL),
        out(QROWS, SEQ),
        out(2, SEQ, BLOCK),
        out(2, SEQ, BLOCK),
    )
    return pl.pallas_call(
        attention_kernel,
        in_specs=[SCALARS]
        + whole(*x, cos, sin, segment)
        + [ANYWHERE] * 5,
        out_specs=(ANYWHERE, ANYWHERE, *whole(*shapes)),
        out_shape=(out(SEQ, MODEL), out(heads, SEQ, SEQ), *shapes),
        scratch_shapes=[
            pltpu.VMEM((QKV, MODEL), BF16),
            pltpu.VMEM((QROWS, MODEL), BF16),
            pltpu.VMEM((SEQ, MODEL), BF16),
            pltpu.VMEM((heads, SEQ, SEQ), BF16),
            pltpu.VMEM((SEQ, SEQ), F32),
            pltpu.SemaphoreType.DMA((16,)),
            pltpu.SemaphoreType.DMA((16,)),
            pltpu.SemaphoreType.DMA((16,)),
            pltpu.SemaphoreType.DMA,
            pltpu.SemaphoreType.DMA((heads,)),
        ],
        compiler_params=params(28),
        cost_estimate=cost(14),
    )(table, *x, cos, sin, segment, *blocks)


def mlp_kernel(table, where, *refs):
    h_in, cot_in, gains, blocks, refs = refs[:8], refs[8:16], refs[16], refs[17:22], refs[22:]
    r_o, n_o, cot_o, act_o, dgu_o, keep_o, send_o = refs[:7]
    w, wd, h, cot, n, act, dgu, chunk, sems, wd_sems, saves = refs[7:]
    copies = fetch(table, blocks, w, sems, 0)
    wd_copies = fetch(table, blocks, wd, wd_sems, 2 * FFN)
    saved = []

    def save(src, dst):
        copy = pltpu.make_async_copy(src, dst, saves.at[len(saved)])
        copy.start()
        saved.append(copy)

    for part in range(2):
        tokens = pl.ds(part * SEQ, SEQ)
        for k in range(4):
            lanes = slice(k * BLOCK, (k + 1) * BLOCK)
            if part == 0:
                lanes = pl.ds(pl.multiple_of(where[k], BLOCK), BLOCK)
            h[:, lanes] = h_in[4 * part + k][...]
            cot[part, :, lanes] = cot_in[4 * part + k][...]
        save(cot.at[part], cot_o.at[tokens])
        hidden = wide(h[...])
        r = lax.rsqrt(jnp.mean(hidden * hidden, -1, keepdims=True) + EPSILON)
        r_o[...] = r
        n[part] = narrow(hidden * r * wide(gains[1:2, :]))
        save(n.at[part], n_o.at[tokens])
        if part == 0:
            wait(copies)
        both = nt(w[...], n[part])
        if part == 0:
            wait(wd_copies)
        d_out = nt(wd[...], cot[part])
        gate, up = both[:FFN], both[FFN:]
        g = jax.nn.sigmoid(gate)
        silu = gate * g
        act[part] = narrow(silu * up)
        save(act.at[part], act_o.at[:, tokens])
        dgu[part, :FFN] = narrow(d_out * up * (g + silu * (1.0 - g)))
        dgu[part, FFN:] = narrow(d_out * silu)
        save(dgu.at[part], dgu_o.at[:, tokens])
        d_n = tn(dgu[part], w[...])
        for k in range(4):
            chunk[4 * part + k] = narrow(d_n[:, k * BLOCK : (k + 1) * BLOCK])
            block = 2 + k // 2 if part else where[4 + k % 2] ^ (k // 2)
            save(chunk.at[4 * part + k], (keep_o, send_o)[k % 2].at[block])
    wait(saved)


def mlp(table, where, h, cot, gains, blocks):
    shapes = (
        out(2 * SEQ, MODEL),
        out(2 * SEQ, MODEL),
        out(FFN, 2 * SEQ),
        out(2 * FFN, 2 * SEQ),
        out(4, SEQ, BLOCK),
        out(4, SEQ, BLOCK),
    )
    return pl.pallas_call(
        mlp_kernel,
        in_specs=[SCALARS] * 2 + whole(*h, *cot, gains) + [ANYWHERE] * 5,
        out_specs=(spec((SEQ, 1)),) + (ANYWHERE,) * 6,
        out_shape=(out(SEQ, 1, dtype=F32), *shapes),
        scratch_shapes=[
            pltpu.VMEM((2 * FFN, MODEL), BF16),
            pltpu.VMEM((FFN, MODEL), BF16),
            pltpu.VMEM((SEQ, MODEL), BF16),
            pltpu.VMEM((2, SEQ, MODEL), BF16),
            pltpu.VMEM((2, SEQ, MODEL), BF16),
            pltpu.VMEM((2, FFN, SEQ), BF16),
            pltpu.VMEM((2, 2 * FFN, SEQ), BF16),
            pltpu.VMEM((8, SEQ, BLOCK), BF16),
            pltpu.SemaphoreType.DMA((16,)),
            pltpu.SemaphoreType.DMA((16,)),
            pltpu.SemaphoreType.DMA((16,)),
        ],
        compiler_params=params(42),
        cost_estimate=cost(30),
    )(table, where, *h, *cot, gains, *blocks)


def down_kernel(table, where, act, *refs):
    blocks, (keep_o, send_o, w, sems) = refs[:5], refs[-4:]
    wait(fetch(table, blocks, w, sems, 2 * FFN))
    value = tn(act[...], w[...])
    for k in range(4):
        lanes = slice(k * BLOCK, (k + 1) * BLOCK)
        to = (keep_o, send_o)[k % 2]
        to[where[4 + k % 2] ^ (k // 2)] = narrow(value[:SEQ, lanes])
        to[2 + k // 2] = narrow(value[SEQ:, lanes])


def down(table, where, act, blocks, after):
    shapes = (out(4, SEQ, BLOCK),) * 2
    return pl.pallas_call(
        down_kernel,
        in_specs=[SCALARS] * 2 + whole(act) + [ANYWHERE] * (5 + len(after)),
        out_specs=tuple(whole(*shapes)),
        out_shape=shapes,
        scratch_shapes=[pltpu.VMEM((FFN, MODEL), BF16), pltpu.SemaphoreType.DMA((16,))],
        compiler_params=params(20),
        cost_estimate=cost(7),
    )(table, where, act, *blocks, *after)


def scatter(table, source, outs, sems, row):
    rows = source.shape[0]
    low, high, one, three, own = outs
    blocks = own, one, low, high, three
    copies = []
    for j in range(4):
        for i in range(4):
            lanes = pl.multiple_of(table[4 * j + i], 128)
            copy = pltpu.make_async_copy(
                source.at[:, pl.ds(lanes, 128)],
                block_of(blocks, j, i).at[pl.ds(row, rows)],
                sems.at[len(copies)],
            )
            copy.start()
            copies.append(copy)
    return copies


def terms_shapes(rows):
    return (out(2, rows, 128),) * 2 + (out(4, rows, 128),) * 3


def grads_mlp_kernel(table, dgu_in, act_in, n_in, cot_in, *refs):
    outs, (dgu, act, n, cot, made, made_down, load_sems, sems, down_sems) = refs[-14:-9], refs[-9:]
    loads = [
        pltpu.make_async_copy(src, dst, load_sems.at[k])
        for k, (src, dst) in enumerate(((dgu_in, dgu), (n_in, n), (act_in, act), (cot_in, cot)))
    ]
    for load in loads:
        load.start()
    wait(loads[:2])
    made[...] = narrow(nn(dgu[...], n[...]))
    copies = scatter(table, made, outs, sems, 0)
    wait(loads[2:])
    made_down[...] = narrow(nn(act[...], cot[...]))
    copies += scatter(table, made_down, outs, down_sems, 2 * FFN)
    wait(copies)


def grads_mlp(table, dgu, act, n, cot, after):
    shapes = terms_shapes(3 * FFN)
    return pl.pallas_call(
        grads_mlp_kernel,
        in_specs=[SCALARS] + [ANYWHERE] * (4 + len(after)),
        out_specs=(ANYWHERE,) * len(shapes),
        out_shape=shapes,
        scratch_shapes=[
            pltpu.VMEM(dgu.shape, BF16),
            pltpu.VMEM(act.shape, BF16),
            pltpu.VMEM(n.shape, BF16),
            pltpu.VMEM(cot.shape, BF16),
            pltpu.VMEM((2 * FFN, MODEL), BF16),
            pltpu.VMEM((FFN, MODEL), BF16),
            pltpu.SemaphoreType.DMA((4,)),
            pltpu.SemaphoreType.DMA((16,)),
            pltpu.SemaphoreType.DMA((16,)),
        ],
        compiler_params=params(34),
        cost_estimate=cost(15),
    )(table, dgu, act, n, cot, *after)


def attention_back_kernel(table, *refs):
    a_in, h_in, cot_in, (r, gains), refs = refs[:4], refs[4:8], refs[8:12], refs[12:14], refs[14:]
    (q, k, v, o, cos, sin), (n_in, p_in), blocks, refs = refs[:6], refs[6:8], refs[8:13], refs[13:]
    x_in, refs = refs[:4], refs[4:]
    (r_one, *_), refs = refs[:1], refs[-27:]
    (dh_o, keep_o, send_o), outs, refs = refs[:3], refs[3:8], refs[8:]
    w, w_qkv, e, n, p, do, dq, dkv, dk, dv, made_out, made = refs[:12]
    w_sems, qkv_sems, out_sems, sems, load_sems, save_sems, chunk = refs[12:]
    qkv_copies = fetch(table, blocks, w_qkv, qkv_sems, 0)
    copies = fetch(table, blocks, w, w_sems, QKV)
    loads = [
        pltpu.make_async_copy(p_in, p, load_sems.at[0]),
        pltpu.make_async_copy(n_in, n, load_sems.at[1]),
    ]
    for load in loads:
        load.start()

    def joined(parts):
        return wide(jnp.concatenate([part[...] for part in parts], 1))

    scale = r[...]
    unit = joined(h_in) * scale
    a = joined(a_in) * wide(gains[1:2, :])
    d_h = joined(cot_in) + scale * (a - unit * jnp.mean(a * unit, -1, keepdims=True))
    dh_o[...] = d_h[:, :BLOCK]
    e[...] = narrow(d_h)
    wait(copies)
    do[...] = narrow(nt(w[...], e[...]))
    made_out[...] = narrow(nn(o[...], e[...]))
    scattered = scatter(table, made_out, outs, out_sems, QKV)

    loads[0].wait()
    dk[...] = jnp.zeros_like(dk)
    dv[...] = jnp.zeros_like(dv)
    for first in range(0, QROWS // HEAD, TOGETHER):
        for start in range(0, SEQ, QUERIES):
            stop = start + QUERIES
            queries = slice(start, stop)
            scores = []
            for h in range(first, first + TOGETHER):
                rows = slice(h * HEAD, (h + 1) * HEAD)
                probs = wide(p[h, :stop, queries])
                dp = tn(v[:, :stop], do[rows, queries])
                scores.append(narrow(probs * (dp - jnp.sum(probs * dp, 0, keepdims=True))))
            for h, ds in zip(range(first, first + TOGETHER), scores, strict=True):
                rows = slice(h * HEAD, (h + 1) * HEAD)
                d_q = nn(k[:, :stop], ds) * SCALE
                dq[rows, queries] = narrow(rotated_back(d_q, cos[:, queries], sin[:, queries]))
                dk[:, :stop] += nt(q[rows, queries], ds)
                dv[:, :stop] += nt(do[rows, queries], p[h, :stop, queries])
    dkv[:HEAD, :] = narrow(rotated_back(dk[...], cos[...], sin[...]))
    dkv[HEAD:, :] = narrow(dv[...])

    loads[1].wait()
    d = jnp.concatenate([dq[...], dkv[...]], 0)
    made[...] = narrow(nn(d, n[...]))
    scattered += scatter(table, made, outs, sems, 0)

    wait(qkv_copies)
    part = tn(d, w_qkv[...])
    product = narrow(part * (joined(x_in) * r_one[...] * wide(gains[0:1, :])))
    stat = narrow(nt(jnp.ones((16, MODEL), BF16), product))
    saved = []
    for k in range(4):
        chunk[k, :SEQ] = narrow(part[:, k * BLOCK : (k + 1) * BLOCK])
        chunk[k, SEQ:] = stat
        to = (keep_o, send_o)[k % 2].at[k // 2]
        saved.append(pltpu.make_async_copy(chunk.at[k], to, save_sems.at[k]))
        saved[-1].start()
    wait(saved)
    wait(scattered)


def attention_back(table, a, h, cot, r, gains, q, k, v, o, cos, sin, n, p, blocks, x, r_one, after):
    heads = QROWS // HEAD
    shapes = (out(SEQ, BLOCK, dtype=F32),)
    chunks = (out(2, SEQ + 16, BLOCK),) * 2
    return pl.pallas_call(
        attention_back_kernel,
        in_specs=[SCALARS]
        + whole(*a, *h, *cot, r, gains, q, k, v, o, cos, sin)
        + [ANYWHERE] * 7
        + whole(*x, r_one)
        + [ANYWHERE] * len(after),
        out_specs=(*whole(*shapes), *[ANYWHERE] * 7),
        out_shape=(*shapes, *chunks, *terms_shapes(GAINS_AT)),
        scratch_shapes=[
            pltpu.VMEM((QROWS, MODEL), BF16),
            pltpu.VMEM((QKV, MODEL), BF16),
            pltpu.VMEM((SEQ, MODEL), BF16),
            pltpu.VMEM((SEQ, MODEL), BF16),
            pltpu.VMEM((heads, SEQ, SEQ), BF16),
            pltpu.VMEM((QROWS, SEQ), BF16),
            pltpu.VMEM((QROWS, SEQ), BF16),
            pltpu.VMEM((2 * HEAD, SEQ), BF16),
            pltpu.VMEM((HEAD, SEQ), F32),
            pltpu.VMEM((HEAD, SEQ), F32),
            pltpu.VMEM((QROWS, MODEL), BF16),
            pltpu.VMEM((QKV, MODEL), BF16),
            pltpu.SemaphoreType.DMA((16,)),
            pltpu.SemaphoreType.DMA((16,)),
            pltpu.SemaphoreType.DMA((16,)),
            pltpu.SemaphoreType.DMA((16,)),
            pltpu.SemaphoreType.DMA((2,)),
            pltpu.SemaphoreType.DMA((4,)),
            pltpu.VMEM((4, SEQ + 16, BLOCK), BF16),
        ],
        compiler_params=params(34),
        cost_estimate=cost(22),
    )(table, *a, *h, *cot, r, gains, q, k, v, o, cos, sin, n, p, *blocks, *x, r_one, *after)


def outputs_kernel(h, m0, m1, m2, m3, dh, c0, c1, x, r, gains, *refs):
    mixed_o, grad_o = refs[-2:]
    m = wide(m0[...]) + wide(m1[...]) + wide(m2[...]) + wide(m3[...])
    mixed_o[...] = narrow(to_natural(h[...] + m))
    total = wide(c0[...]) + wide(c1[...])
    stat = total[SEQ:].T[:, :1] * (1.0 / MODEL)
    scale = r[...]
    c_full = total[:SEQ] * wide(gains[0:1, :])
    grad_o[...] = to_natural(dh[...] + scale * (c_full - wide(x[...]) * scale * stat))


def outputs(h, m, dh, c, x, r, gains, after):
    shapes = (out(SEQ, BLOCK), out(SEQ, BLOCK, dtype=F32))
    args = (h, *m, dh, *c, x, r)
    return pl.pallas_call(
        outputs_kernel,
        grid=(1,),
        in_specs=whole(*args) + [spec((GAINS, BLOCK))] + [ANYWHERE] * len(after),
        out_specs=tuple(whole(*shapes)),
        out_shape=shapes,
        compiler_params=params(),
        cost_estimate=cost(5),
    )(*args, gains, *after)


def spread_eight(own, opposite, first, second):
    return own, cross(False)(first), cross(True)(second), swap_xh(opposite)


def gather_four(v):
    other = swap_xh(v)
    return v, swap_core(v), other, swap_core(other)


def gather_other(v):
    first, second = cross(False), cross(True)
    a, b = first(v), second(v)
    return (a, swap_core(a), b, swap_core(b)), second(a)


def gather_own(v, opposite):
    return v, swap_core(v), opposite, swap_core(opposite)


def shards(
    tokens,
    w_query,
    key_value_weight,
    w_output,
    w_gate,
    w_up,
    w_down,
    gain_attention,
    gain_mlp,
    segment,
    position,
    cotangent,
):
    core = lax.axis_index("core")
    col = lax.axis_index("xh") * 2 + core
    upper = lax.axis_index("xl") == 1
    far, close = jnp.arange(4)[:, None], jnp.arange(4)[None, :]
    y = (lax.axis_index("y") ^ col) ^ jnp.where(core == 0, far, close)
    z = lax.axis_index("z") ^ jnp.where(core == 0, close, far)
    table = ((y * 4 + z) * 128).reshape(16).astype(jnp.int32)
    other_at = jnp.stack(
        [
            2 * BLOCK * core,
            BLOCK + 2 * BLOCK * (1 - core),
            2 * BLOCK * (1 - core),
            BLOCK + 2 * BLOCK * core,
            core,
            1 - core,
            lax.axis_index("xl"),
        ]
    ).astype(jnp.int32)

    x_own, cot_own, attn_rows = prepare(
        tokens, cotangent, w_query, key_value_weight, w_output.T, gain_attention, gain_mlp
    )
    mlp_keep, mlp_pack = prepare_mlp(other_at, w_gate, w_up, w_down.T)
    attn_shard = shard_attention(other_at, attn_rows, swap_xl(attn_rows), (mlp_pack,))
    x_all = gather_four(x_own)
    attn_blocks = gather_two(attn_shard, (mlp_pack,))
    mlp_shard = merge(
        other_at, mlp_keep, swap_xl(mlp_pack), (attn_blocks[1], attn_blocks[4])
    )
    cot_other, opposite = gather_other(cot_own)
    cot_self = gather_own(cot_own, opposite)

    frequency = jnp.exp(jnp.arange(HALF).astype(F32) * (-2.0 * math.log(10000.0) / HEAD))
    angles = frequency[:, None] * position.astype(F32)[None, :]
    cos, sin = jnp.cos(angles), jnp.sin(angles)
    normed_one, probs, r_one, q, k, v, gains, o, keep, send = attention(
        table, x_all, cos, sin, segment[None, :], attn_blocks
    )
    here, there = add_cores(keep, send)
    resid = wide(x_own) + wide(here) + wide(swap_xh(there))
    resid_low = narrow(resid)
    mlp_blocks = gather_two(mlp_shard, (r_one,))
    h_other, opposite = gather_other(resid_low)
    h_self = gather_own(resid_low, opposite)
    r_two, n, cot, act, dgu, keep, send = mlp(
        table, other_at, (*h_other, *h_self), (*cot_other, *cot_self), gains, mlp_blocks
    )
    sums = add_cores(keep, send)
    mlp_terms = grads_mlp(table, dgu, act, n, cot, sums[:1])
    d_normed_two = sum_terms(spread_eight(sums[2], sums[3], sums[0], sums[1]))
    mlp_terms = tie(mlp_terms, d_normed_two)
    keep, send = down(table, other_at, act, mlp_blocks, (d_normed_two,))
    (opposite,) = tie((swap_xh(d_normed_two),), keep)
    keep, send = tie((keep, send), opposite)
    d_normed_all = gather_own(d_normed_two, opposite)
    mlp_terms = reduce_start(mlp_terms, ())
    sum_out = add_cores(keep, send)
    mlp_out = spread_eight(sum_out[2], sum_out[3], sum_out[0], sum_out[1])
    d_resid, keep, send, *attn_terms = attention_back(
        table,
        d_normed_all,
        h_self,
        cot_self,
        r_two,
        gains,
        q,
        k,
        v,
        o,
        cos,
        sin,
        normed_one,
        probs,
        attn_blocks,
        x_all,
        r_one,
        mlp_terms[:1],
    )
    here, there = add_cores(keep, send)

    d_normed_one = here, swap_xh(there)
    mlp_parts = reduce_end(*mlp_terms, ())
    attn_terms = reduce_start(attn_terms, (here, mlp_parts[0]))
    attn_parts = reduce_end(*attn_terms, d_normed_one[1:])
    mlp_total, mlp_pack = sum_pack(other_at, mlp_parts, attn_terms[:1])
    mixed, input_grad = outputs(
        resid, mlp_out, d_resid, d_normed_one, x_own, r_one, gains, attn_parts[:1]
    )
    attn_total, attn_pack = sum_pack(other_at, attn_parts, (mixed,))
    grad_gate, grad_up, grad_down, sum_two = finish_mlp(
        other_at, mlp_total, swap_xl(mlp_pack), w_gate, w_up
    )
    grad_query, grad_keyval, grad_output, sum_one = finish_attention(
        other_at, attn_total, swap_xl(attn_pack), w_query, key_value_weight
    )
    sums = jnp.concatenate([sum_one, sum_two], 0).reshape(1, 128)
    sums = (sums + swap_core(sums) + swap_xh(sums) + swap_both(sums)).reshape(2, 64)
    gain_one = sums[0] / wide(gain_attention)
    gain_two = sums[1] / wide(gain_mlp)
    return (
        mixed,
        input_grad,
        grad_query,
        grad_keyval,
        grad_output.T,
        grad_gate,
        grad_up,
        grad_down.T,
        gain_one,
        gain_two,
    )


def solution(mesh):
    fine = Mesh(mesh.devices.reshape(SIZES), AXES)
    both, turned, rows = P(ROW, COL), P(COL, ROW), P(ROW)
    return jax.shard_map(
        shards,
        mesh=fine,
        in_specs=(both, both, both, turned, both, both, turned, rows, rows, rows, rows, both),
        out_specs=(both, both, both, both, turned, both, both, turned, rows, rows),
        check_vma=False,
    )
```

```python
import functools
import math

import jax
import jax.numpy as jnp
from jax import lax
from jax.experimental import pallas as pl
from jax.experimental.pallas import tpu as pltpu
from jax.sharding import Mesh, PartitionSpec as P

F32, BF16 = jnp.float32, jnp.bfloat16
HEAD = 64
HALF = HEAD // 2
SCALE = 1.0 / math.sqrt(HEAD)
EPSILON = 1e-05
MASKED = -1e30
AXES = ("y", "xl", "z", "xh", "core")
SIZES = (4, 2, 4, 2, 2)
ROW, COL = ("y", "xl", "z"), ("xh", "core")

SEQ = 512
QUERIES = 256
TOGETHER = 4
MODEL = 2048
BLOCK = 512
QROWS = 512
QKV = QROWS + 128
GAINS_AT = QKV + 512
GAINS = 32
FFN = 704


def turn(second, mask):
    pairs = []
    for i in range(32):
        shift = 1 if (i % 2 == 0) != second else 3
        pairs.append((i, i ^ (mask << shift)))
    return lambda v: lax.ppermute(v, ("y", "z", "core"), pairs)


def cross(second):
    pairs = []
    for i in range(8):
        near = (i % 2 == 0) != second
        pairs.append((i, i ^ (4 if near else 6)))
    return lambda v: lax.ppermute(v, ("xl", "xh", "core"), pairs)


def swap_core(v):
    return lax.ppermute(v, "core", [(0, 1), (1, 0)])


def swap_xh(v):
    return lax.ppermute(v, "xh", [(0, 1), (1, 0)])


def swap_both(v):
    return lax.ppermute(v, ("xh", "core"), [(i, i ^ 3) for i in range(4)])


def swap_xl(v):
    return lax.ppermute(v, "xl", [(0, 1), (1, 0)])


def narrow(v):
    return v.astype(BF16)


def wide(v):
    return v.astype(F32)


def gather_two(v, after):
    held = bundle([v] + [turn(False, mask)(v) for mask in (1, 2, 3)], after)
    near, far = turn(True, 1), turn(True, 3)
    from_near, from_far = near(held), far(held)
    first, last = halves(from_near, from_far)
    return held, from_near, far(first), near(last), from_far


def reduce_start(terms, after):
    low, high, one, three, own = terms
    return (*add_halves(one, three, turn(True, 1)(low), turn(True, 3)(high), after), own)


def reduce_end(one, three, own, after):
    parts = sum_blocks(own, turn(True, 1)(one), turn(True, 3)(three), after)
    return [parts[0]] + [turn(False, mask)(parts[mask]) for mask in (1, 2, 3)]


def dot(a, b, contract):
    return lax.dot_general(a, b, ((contract[:1], contract[1:]), ((), ())), preferred_element_type=F32)


def nn(a, b):
    return dot(a, b, (1, 0))


def nt(a, b):
    return dot(a, b, (1, 1))


def tn(a, b):
    return dot(a, b, (0, 0))


def params(mib=14):
    return pltpu.CompilerParams(vmem_limit_bytes=mib * 1024 * 1024)


def cost(us):
    return pl.CostEstimate(flops=int(us * 1.15e9), bytes_accessed=0, transcendentals=0)


def spec(shape, index=None):
    zeros = (0,) * len(shape)
    return pl.BlockSpec(shape, index if index is not None else (lambda *_: zeros))


def held_by(arrays):
    return [a[0] if isinstance(a, tuple) else a for a in arrays]


def whole(*arrays):
    return [spec(a.shape) for a in held_by(arrays)]


def views(refs, k):
    return [ref.at[k] if len(ref.shape) == 3 else ref for ref in refs]


def out(*shape, dtype=BF16):
    return jax.ShapeDtypeStruct(shape, dtype)


def lane_low(shape):
    return lax.broadcasted_iota(jnp.int32, shape, 1) < 64


def pair(a, b):
    low = lane_low(a.shape)
    return jnp.where(low, a, pltpu.roll(b, 64, 1)), jnp.where(low, pltpu.roll(a, 64, 1), b)


def tie_kernel(*refs):
    pass


def tie(arrays, *after):
    count = len(arrays)
    return pl.pallas_call(
        tie_kernel,
        in_specs=[ANYWHERE] * (count + len(after)),
        out_specs=(ANYWHERE,) * count,
        out_shape=tuple(jax.ShapeDtypeStruct(v.shape, v.dtype) for v in arrays),
        input_output_aliases={k: k for k in range(count)},
        compiler_params=params(),
        cost_estimate=cost(1),
    )(*arrays, *after)


def inner(src, dst):
    t = [wide(src[:, k * 128 : (k + 1) * 128]) for k in range(4)]
    z0, z1 = pair(t[0], t[2])
    z2, z3 = pair(t[1], t[3])
    for k, value in enumerate((z0, z1, z2, z3)):
        dst[:, k * 128 : (k + 1) * 128] = narrow(value)


def column(row):
    n = row.shape[1]
    here = lax.broadcasted_iota(jnp.int32, (n, n), 0) == lax.broadcasted_iota(jnp.int32, (n, n), 1)
    return jnp.sum(jnp.where(here, wide(row[...]), 0.0), 1, keepdims=True)


def prepare_kernel(tokens, cot, w_q, w_kv, w_o, gain_a, gain_m, x_o, cot_o, rows_o):
    rows_o[:, :QROWS] = w_q[...]
    rows_o[:, QROWS:QKV] = w_kv[...]
    rows_o[:, QKV:GAINS_AT] = w_o[...]
    lane = lax.broadcasted_iota(jnp.int32, (64, GAINS), 1)
    gains = jnp.where(lane == 0, column(gain_a), jnp.where(lane == 1, column(gain_m), 0.0))
    rows_o[:, GAINS_AT:] = narrow(gains)
    inner(tokens, x_o)
    inner(cot, cot_o)


def prepare(tokens, cot, w_q, w_kv, w_o, gain_a, gain_m):
    shapes = (out(*tokens.shape), out(*cot.shape), out(64, GAINS_AT + GAINS))
    args = (tokens, cot, w_q, w_kv, w_o, gain_a[None, :], gain_m[None, :])
    return pl.pallas_call(
        prepare_kernel,
        in_specs=whole(*args),
        out_specs=tuple(whole(*shapes)),
        out_shape=shapes,
        compiler_params=params(),
        cost_estimate=cost(3),
    )(*args)


def shard_attention_kernel(where, mine, other, *refs):
    upper = where[6] == 1
    a, b = wide(mine[...]), wide(other[...])
    rows = jnp.concatenate([jnp.where(upper, b, a), jnp.where(upper, a, b)], 0)
    refs[-1][...] = narrow(rows.T)


def shard_attention(where, mine, other, after):
    shape = out(mine.shape[1], 128)
    return pl.pallas_call(
        shard_attention_kernel,
        in_specs=[SCALARS] + whole(mine, other) + [ANYWHERE] * len(after),
        out_specs=spec(shape.shape),
        out_shape=shape,
        compiler_params=params(),
        cost_estimate=cost(2),
    )(where, mine, other, *after)


def prepare_mlp_kernel(where, w_g, w_u, w_d, keep_o, pack_o, held):
    for k, w in enumerate((w_g, w_u, w_d)):
        value = wide(w[...])
        both = jnp.concatenate([value[:, :FFN], value[:, FFN:]], 0)
        held[k * FFN : (k + 1) * FFN] = both.T
    keep_o[...] = narrow(held[...])
    pack_o[...] = narrow(packed(held[...], where[6] == 1))


def prepare_mlp(where, w_g, w_u, w_d):
    rows = 3 * FFN
    shapes = (out(rows, 128), out(rows // 2, 128))
    return pl.pallas_call(
        prepare_mlp_kernel,
        in_specs=[SCALARS] + whole(w_g, w_u, w_d),
        out_specs=tuple(whole(*shapes)),
        out_shape=shapes,
        scratch_shapes=[pltpu.VMEM((rows, 128), F32)],
        compiler_params=params(),
        cost_estimate=cost(4),
    )(where, w_g, w_u, w_d)


def sum_terms_kernel(a, b, c, d, total_o):
    total_o[...] = narrow(wide(a[...]) + wide(b[...]) + wide(c[...]) + wide(d[...]))


def sum_terms(terms):
    shape = out(*terms[0].shape)
    return pl.pallas_call(
        sum_terms_kernel,
        in_specs=whole(*terms),
        out_specs=spec(shape.shape),
        out_shape=shape,
        compiler_params=params(),
        cost_estimate=cost(2),
    )(*terms)


def add_split_kernel(a, b, *outs):
    for k, ref in enumerate(outs):
        ref[...] = narrow(wide(a[k]) + wide(b[k]))


def add_cores(keep, send):
    shapes = (out(*keep.shape[1:]),) * keep.shape[0]
    return pl.pallas_call(
        add_split_kernel,
        in_specs=whole(keep, send),
        out_specs=tuple(whole(*shapes)),
        out_shape=shapes,
        compiler_params=params(),
        cost_estimate=cost(2),
    )(keep, swap_core(send))


def add_two_kernel(a, b, total_o):
    total_o[...] = narrow(wide(a[...]) + wide(b[1]))


def add_two(a, b):
    return pl.pallas_call(
        add_two_kernel,
        in_specs=whole(a, b),
        out_specs=spec(a.shape),
        out_shape=out(*a.shape),
        compiler_params=params(),
        cost_estimate=cost(1),
    )(*held_by((a, b)))


def add_paired_kernel(a, b, pair_o, second_o, own_o):
    total = lambda k: narrow(wide(a[k]) + wide(b[k]))
    pair_o[0] = total(0)
    second_o[...] = total(1)
    own_o[...] = total(2)
    pair_o[1] = total(3)


def add_cores_paired(keep, send):
    block = out(*keep.shape[1:])
    shapes = (out(2, *keep.shape[1:]), block, block)
    return pl.pallas_call(
        add_paired_kernel,
        in_specs=whole(keep, send),
        out_specs=tuple(whole(*shapes)),
        out_shape=shapes,
        compiler_params=params(),
        cost_estimate=cost(3),
    )(keep, swap_core(send))


def to_natural(v):
    z = [v[:, k * 128 : (k + 1) * 128] for k in range(4)]
    t0, t2 = pair(z[0], z[1])
    t1, t3 = pair(z[2], z[3])
    return jnp.concatenate([t0, t1, t2, t3], 1)


def fetch(table, blocks, target, sems, start):
    rows = target.shape[0]
    copies = []
    for j in range(4):
        for i in range(4):
            src = block_of(blocks, j, i)
            lanes = pl.multiple_of(table[4 * j + i], 128)
            copy = pltpu.make_async_copy(
                src.at[pl.ds(start, rows)], target.at[:, pl.ds(lanes, 128)], sems.at[len(copies)]
            )
            copy.start()
            copies.append(copy)
    return copies


def block_of(blocks, j, i):
    own, one, low, high, three = blocks
    if j == 2:
        return low.at[i] if i < 2 else high.at[i - 2]
    return (own, one, None, three)[j].at[i]


def wait(copies):
    for copy in copies:
        copy.wait()


ANYWHERE = pl.BlockSpec(memory_space=pl.ANY)
SCALARS = pl.BlockSpec(memory_space=pltpu.SMEM)


def halves_kernel(a, b, a_o, b_o):
    a_o[...] = a[...]
    b_o[...] = b[...]


def halves(a, b):
    block = (2,) + a.shape[1:]
    first = spec(block, lambda i: (0, 0, 0))
    return pl.pallas_call(
        halves_kernel,
        grid=(1,),
        in_specs=[first, spec(block, lambda i: (1, 0, 0))],
        out_specs=(first, first),
        out_shape=(out(*block),) * 2,
        compiler_params=params(),
        cost_estimate=cost(2),
    )(a, b)


def add_halves_kernel(one, three, low, high, *refs):
    one_o, three_o = refs[-2:]
    three_o[...] = narrow(wide(three[...]) + wide(low[...]))
    one_o[...] = narrow(wide(one[...]) + wide(high[...]))


def add_halves(one, three, low, high, after):
    block = (1,) + one.shape[1:]
    first, last = spec(block, lambda i: (i, 0, 0)), spec(block, lambda i: (2 + i, 0, 0))
    return pl.pallas_call(
        add_halves_kernel,
        grid=(2,),
        in_specs=[last, first, first, first] + [ANYWHERE] * len(after),
        out_specs=(last, first),
        out_shape=(out(*one.shape),) * 2,
        input_output_aliases={0: 0, 1: 1},
        compiler_params=params(),
        cost_estimate=cost(2),
    )(one, three, low, high, *after)


def sum_blocks_kernel(a, b, c, *refs):
    for k, ref in enumerate(refs[-4:]):
        ref[...] = narrow(wide(a[k]) + wide(b[k]) + wide(c[k]))


def sum_blocks(a, b, c, after):
    shapes = (out(*a.shape[1:]),) * 4
    return pl.pallas_call(
        sum_blocks_kernel,
        in_specs=whole(a, b, c) + [ANYWHERE] * len(after),
        out_specs=tuple(whole(*shapes)),
        out_shape=shapes,
        compiler_params=params(),
        cost_estimate=cost(3),
    )(a, b, c, *after)


def packed(v, upper):
    half = v.shape[0] // 2
    top, bottom = v[:half], v[half:]
    low = lane_low(top.shape)
    return jnp.where(
        upper,
        jnp.where(low, top, pltpu.roll(bottom, 64, 1)),
        jnp.where(low, pltpu.roll(top, 64, 1), bottom),
    )


def unpacked(v, upper):
    turned = pltpu.roll(v, 64, 1)
    return [jnp.where(upper, v, turned), jnp.where(upper, turned, v)]


def own_lanes(shape, upper):
    return lane_low(shape) != upper


def sum_pack_kernel(where, *refs, count):
    sum_o, pack_o = refs[-2:]
    total = wide(refs[0][...])
    for ref in refs[1:count]:
        total += wide(ref[...])
    sum_o[...] = total
    pack_o[...] = narrow(packed(total, where[6] == 1))


def sum_pack(where, parts, after):
    rows = parts[0].shape[0]
    shapes = (out(rows, 128, dtype=F32), out(rows // 2, 128))
    return pl.pallas_call(
        functools.partial(sum_pack_kernel, count=len(parts)),
        in_specs=[SCALARS] + whole(*parts) + [ANYWHERE] * len(after),
        out_specs=tuple(whole(*shapes)),
        out_shape=shapes,
        compiler_params=params(),
        cost_estimate=cost(2),
    )(where, *parts, *after)


def merge_kernel(where, keep, other, *refs):
    upper = where[6] == 1
    half = other.shape[0]
    for k, part in enumerate(unpacked(wide(other[...]), upper)):
        rows = slice(k * half, (k + 1) * half)
        refs[-1][rows] = narrow(
            jnp.where(own_lanes(part.shape, upper), wide(keep[rows, :]), part)
        )


def merge(where, keep, other, after):
    return pl.pallas_call(
        merge_kernel,
        in_specs=[SCALARS] + whole(keep, other) + [ANYWHERE] * len(after),
        out_specs=spec(keep.shape),
        out_shape=out(*keep.shape),
        compiler_params=params(),
        cost_estimate=cost(2),
    )(where, keep, other, *after)


def row_dot(weight, grad):
    return jnp.sum(wide(weight) * grad, -1, keepdims=True)


def finish_mlp_kernel(where, total, other, w_gate, w_up, gate_o, up_o, down_o, sum_o, held):
    upper = where[6] == 1
    half = other.shape[0]
    for k, part in enumerate(unpacked(wide(other[...]), upper)):
        rows = slice(k * half, (k + 1) * half)
        held[rows] = jnp.where(own_lanes(part.shape, upper), total[rows, :], part)
    for k, ref in enumerate((gate_o, up_o, down_o)):
        turned = held[k * FFN : (k + 1) * FFN].T
        ref[:, :FFN] = turned[:64]
        ref[:, FFN:] = turned[64:]
    sum_o[...] = row_dot(w_gate[...], gate_o[...]) + row_dot(w_up[...], up_o[...])


def finish_mlp(where, total, other, w_gate, w_up):
    shapes = (out(64, 2 * FFN, dtype=F32),) * 3 + (out(64, 1, dtype=F32),)
    return pl.pallas_call(
        finish_mlp_kernel,
        in_specs=[SCALARS] + whole(total, other, w_gate, w_up),
        out_specs=tuple(whole(*shapes)),
        out_shape=shapes,
        scratch_shapes=[pltpu.VMEM(total.shape, F32)],
        compiler_params=params(),
        cost_estimate=cost(4),
    )(where, total, other, w_gate, w_up)


def finish_attention_kernel(where, total, other, w_q, w_kv, q_o, kv_o, out_o, sum_o, held):
    upper = where[6] == 1
    half = other.shape[0]
    for k, part in enumerate(unpacked(wide(other[...]), upper)):
        rows = slice(k * half, (k + 1) * half)
        held[:, rows] = (total[rows, :] + pltpu.roll(part, 64, 1)).T
    mine = held[pl.ds(pl.multiple_of(where[6] * 64, 64), 64), :]
    q_o[...] = mine[:, :QROWS]
    kv_o[...] = mine[:, QROWS:QKV]
    out_o[...] = mine[:, QKV:]
    sum_o[...] = row_dot(w_q[...], q_o[...]) + row_dot(w_kv[...], kv_o[...])


def finish_attention(where, total, other, w_q, w_kv):
    shapes = tuple(out(64, n, dtype=F32) for n in (QROWS, QKV - QROWS, QROWS, 1))
    return pl.pallas_call(
        finish_attention_kernel,
        in_specs=[SCALARS] + whole(total, other, w_q, w_kv),
        out_specs=tuple(whole(*shapes)),
        out_shape=shapes,
        scratch_shapes=[pltpu.VMEM((128, total.shape[0]), F32)],
        compiler_params=params(),
        cost_estimate=cost(3),
    )(where, total, other, w_q, w_kv)


def rotated(v, cos, sin):
    a, b = v[:HALF], v[HALF:]
    return jnp.concatenate([a * cos - b * sin, b * cos + a * sin], 0)


def rotated_back(v, cos, sin):
    a, b = v[:HALF], v[HALF:]
    return jnp.concatenate([a * cos + b * sin, b * cos - a * sin], 0)


def bundle_kernel(*refs, count):
    for k in range(count):
        refs[-1][k] = refs[k][...]


def bundle(parts, after):
    shape = out(len(parts), *parts[0].shape)
    return pl.pallas_call(
        functools.partial(bundle_kernel, count=len(parts)),
        in_specs=whole(*parts) + [ANYWHERE] * len(after),
        out_specs=spec(shape.shape),
        out_shape=shape,
        compiler_params=params(),
        cost_estimate=cost(2),
    )(*parts, *after)


def attention_kernel(table, x0, x1, x2, x3, cos, sin, segment, *refs):
    blocks, refs = refs[:5], refs[-20:]
    n_o, p_o, r_o, q_o, k_o, v_o, gains_o, o_o, keep_o, send_o = refs[:10]
    w, w_out, n, probs, bias, w_sems, out_sems, gain_sems, n_sem, p_sems = refs[10:]
    copies = fetch(table, blocks, gains_o, gain_sems, GAINS_AT)
    w_copies = fetch(table, blocks, w, w_sems, 0)
    out_copies = fetch(table, blocks, w_out, out_sems, QKV)
    x = wide(jnp.concatenate([x0[...], x1[...], x2[...], x3[...]], 1))
    r = lax.rsqrt(jnp.mean(x * x, -1, keepdims=True) + EPSILON)
    r_o[...] = r
    wait(copies)
    n[...] = narrow(x * r * wide(gains_o[0:1, :]))
    saved = [pltpu.make_async_copy(n, n_o, n_sem)]
    saved[0].start()

    shape = (SEQ, SEQ)
    key = lax.broadcasted_iota(jnp.int32, shape, 0)
    query = lax.broadcasted_iota(jnp.int32, shape, 1)
    allowed = (column(segment) == wide(segment[...])) & (key <= query)
    bias[...] = jnp.where(allowed, 0.0, MASKED)

    wait(w_copies)
    qkv = nt(w[...], n[...])
    c, s = cos[...], sin[...]
    for h in range(QROWS // HEAD):
        head = rotated(qkv[h * HEAD : (h + 1) * HEAD], c, s)
        q_o[h * HEAD : (h + 1) * HEAD, :] = narrow(head) * SCALE
    k_o[...] = narrow(rotated(qkv[QROWS : QROWS + HEAD], c, s))
    v_o[...] = narrow(qkv[QROWS + HEAD :])

    for first in range(0, QROWS // HEAD, TOGETHER):
        for start in range(0, SEQ, QUERIES):
            stop = start + QUERIES
            queries = slice(start, stop)
            for h in range(first, first + TOGETHER):
                rows = slice(h * HEAD, (h + 1) * HEAD)
                s = tn(k_o[:, :stop], q_o[rows, queries]) + bias[:stop, queries]
                e = jnp.exp(s - jnp.max(s, 0, keepdims=True))
                probs[h, :stop, queries] = narrow(e * (1.0 / jnp.sum(e, 0, keepdims=True)))
            for h in range(first, first + TOGETHER):
                rows = slice(h * HEAD, (h + 1) * HEAD)
                o_o[rows, queries] = narrow(nn(v_o[:, :stop], probs[h, :stop, queries]))
        some = pl.ds(first, TOGETHER)
        saved.append(pltpu.make_async_copy(probs.at[some], p_o.at[some], p_sems.at[first]))
        saved[-1].start()

    wait(out_copies)
    value = tn(o_o[...], w_out[...])
    for k in range(4):
        (keep_o, send_o)[k % 2][k // 2] = narrow(value[:, k * BLOCK : (k + 1) * BLOCK])
    wait(saved)


def attention(table, x, cos, sin, segment, blocks):
    heads = QROWS // HEAD
    shapes = (
        out(SEQ, 1, dtype=F32),
        out(QROWS, SEQ),
        out(HEAD, SEQ),
        out(HEAD, SEQ),
        out(GAINS, MODEL),
        out(QROWS, SEQ),
        out(2, SEQ, BLOCK),
        out(2, SEQ, BLOCK),
    )
    return pl.pallas_call(
        attention_kernel,
        in_specs=[SCALARS]
        + whole(*x, cos, sin, segment)
        + [ANYWHERE] * 5,
        out_specs=(ANYWHERE, ANYWHERE, *whole(*shapes)),
        out_shape=(out(SEQ, MODEL), out(heads, SEQ, SEQ), *shapes),
        scratch_shapes=[
            pltpu.VMEM((QKV, MODEL), BF16),
            pltpu.VMEM((QROWS, MODEL), BF16),
            pltpu.VMEM((SEQ, MODEL), BF16),
            pltpu.VMEM((heads, SEQ, SEQ), BF16),
            pltpu.VMEM((SEQ, SEQ), F32),
            pltpu.SemaphoreType.DMA((16,)),
            pltpu.SemaphoreType.DMA((16,)),
            pltpu.SemaphoreType.DMA((16,)),
            pltpu.SemaphoreType.DMA,
            pltpu.SemaphoreType.DMA((heads,)),
        ],
        compiler_params=params(28),
        cost_estimate=cost(14),
    )(table, *x, cos, sin, segment, *blocks)


def mlp_kernel(table, where, *refs):
    h_in, cot_in = (views(refs[k : k + 4], 0) + views(refs[k + 4 : k + 8], 1) for k in (0, 8))
    gains, blocks, refs = refs[16], refs[17:22], refs[22:]
    r_o, n_o, cot_o, act_o, dgu_o, keep_o, send_o = refs[:7]
    w, wd, h, cot, n, act, dgu, chunk, sems, wd_sems, saves = refs[7:]
    copies = fetch(table, blocks, w, sems, 0)
    wd_copies = fetch(table, blocks, wd, wd_sems, 2 * FFN)
    saved = []

    def save(src, dst):
        copy = pltpu.make_async_copy(src, dst, saves.at[len(saved)])
        copy.start()
        saved.append(copy)

    for part in range(2):
        tokens = pl.ds(part * SEQ, SEQ)
        for k in range(4):
            lanes = slice(k * BLOCK, (k + 1) * BLOCK)
            if part == 0:
                lanes = pl.ds(pl.multiple_of(where[k], BLOCK), BLOCK)
            h[:, lanes] = h_in[4 * part + k][...]
            cot[part, :, lanes] = cot_in[4 * part + k][...]
        save(cot.at[part], cot_o.at[tokens])
        hidden = wide(h[...])
        r = lax.rsqrt(jnp.mean(hidden * hidden, -1, keepdims=True) + EPSILON)
        r_o[...] = r
        n[part] = narrow(hidden * r * wide(gains[1:2, :]))
        save(n.at[part], n_o.at[tokens])
        if part == 0:
            wait(copies)
        both = nt(w[...], n[part])
        if part == 0:
            wait(wd_copies)
        d_out = nt(wd[...], cot[part])
        gate, up = both[:FFN], both[FFN:]
        g = jax.nn.sigmoid(gate)
        silu = gate * g
        act[part] = narrow(silu * up)
        save(act.at[part], act_o.at[:, tokens])
        dgu[part, :FFN] = narrow(d_out * up * (g + silu * (1.0 - g)))
        dgu[part, FFN:] = narrow(d_out * silu)
        save(dgu.at[part], dgu_o.at[:, tokens])
        d_n = tn(dgu[part], w[...])
        for k in range(4):
            chunk[4 * part + k] = narrow(d_n[:, k * BLOCK : (k + 1) * BLOCK])
            block = 2 + k // 2 if part else where[4 + k % 2] ^ (k // 2)
            save(chunk.at[4 * part + k], (keep_o, send_o)[k % 2].at[block])
    wait(saved)


def mlp(table, where, h, cot, gains, blocks):
    shapes = (
        out(2 * SEQ, MODEL),
        out(2 * SEQ, MODEL),
        out(FFN, 2 * SEQ),
        out(2 * FFN, 2 * SEQ),
        out(4, SEQ, BLOCK),
        out(4, SEQ, BLOCK),
    )
    return pl.pallas_call(
        mlp_kernel,
        in_specs=[SCALARS] * 2 + whole(*h, *cot, gains) + [ANYWHERE] * 5,
        out_specs=(spec((SEQ, 1)),) + (ANYWHERE,) * 6,
        out_shape=(out(SEQ, 1, dtype=F32), *shapes),
        scratch_shapes=[
            pltpu.VMEM((2 * FFN, MODEL), BF16),
            pltpu.VMEM((FFN, MODEL), BF16),
            pltpu.VMEM((SEQ, MODEL), BF16),
            pltpu.VMEM((2, SEQ, MODEL), BF16),
            pltpu.VMEM((2, SEQ, MODEL), BF16),
            pltpu.VMEM((2, FFN, SEQ), BF16),
            pltpu.VMEM((2, 2 * FFN, SEQ), BF16),
            pltpu.VMEM((8, SEQ, BLOCK), BF16),
            pltpu.SemaphoreType.DMA((16,)),
            pltpu.SemaphoreType.DMA((16,)),
            pltpu.SemaphoreType.DMA((16,)),
        ],
        compiler_params=params(42),
        cost_estimate=cost(30),
    )(table, where, *held_by((*h, *cot)), gains, *blocks)


def down_kernel(table, where, act, *refs):
    blocks, (keep_o, send_o, w, sems) = refs[:5], refs[-4:]
    wait(fetch(table, blocks, w, sems, 2 * FFN))
    value = tn(act[...], w[...])
    for k in range(4):
        lanes = slice(k * BLOCK, (k + 1) * BLOCK)
        to = (keep_o, send_o)[k % 2]
        to[where[4 + k % 2] ^ (k // 2)] = narrow(value[:SEQ, lanes])
        to[2 + k // 2] = narrow(value[SEQ:, lanes])


def down(table, where, act, blocks, after):
    shapes = (out(4, SEQ, BLOCK),) * 2
    return pl.pallas_call(
        down_kernel,
        in_specs=[SCALARS] * 2 + whole(act) + [ANYWHERE] * (5 + len(after)),
        out_specs=tuple(whole(*shapes)),
        out_shape=shapes,
        scratch_shapes=[pltpu.VMEM((FFN, MODEL), BF16), pltpu.SemaphoreType.DMA((16,))],
        compiler_params=params(20),
        cost_estimate=cost(7),
    )(table, where, act, *blocks, *after)


def scatter(table, source, outs, sems, row):
    rows = source.shape[0]
    low, high, one, three, own = outs
    blocks = own, one, low, high, three
    copies = []
    for j in range(4):
        for i in range(4):
            lanes = pl.multiple_of(table[4 * j + i], 128)
            copy = pltpu.make_async_copy(
                source.at[:, pl.ds(lanes, 128)],
                block_of(blocks, j, i).at[pl.ds(row, rows)],
                sems.at[len(copies)],
            )
            copy.start()
            copies.append(copy)
    return copies


def terms_shapes(rows):
    return (out(2, rows, 128),) * 2 + (out(4, rows, 128),) * 3


def grads_mlp_kernel(table, dgu_in, act_in, n_in, cot_in, *refs):
    outs, (dgu, act, n, cot, made, made_down, load_sems, sems, down_sems) = refs[-14:-9], refs[-9:]
    loads = [
        pltpu.make_async_copy(src, dst, load_sems.at[k])
        for k, (src, dst) in enumerate(((dgu_in, dgu), (n_in, n), (act_in, act), (cot_in, cot)))
    ]
    for load in loads:
        load.start()
    wait(loads[:2])
    made[...] = narrow(nn(dgu[...], n[...]))
    copies = scatter(table, made, outs, sems, 0)
    wait(loads[2:])
    made_down[...] = narrow(nn(act[...], cot[...]))
    copies += scatter(table, made_down, outs, down_sems, 2 * FFN)
    wait(copies)


def grads_mlp(table, dgu, act, n, cot, after):
    shapes = terms_shapes(3 * FFN)
    return pl.pallas_call(
        grads_mlp_kernel,
        in_specs=[SCALARS] + [ANYWHERE] * (4 + len(after)),
        out_specs=(ANYWHERE,) * len(shapes),
        out_shape=shapes,
        scratch_shapes=[
            pltpu.VMEM(dgu.shape, BF16),
            pltpu.VMEM(act.shape, BF16),
            pltpu.VMEM(n.shape, BF16),
            pltpu.VMEM(cot.shape, BF16),
            pltpu.VMEM((2 * FFN, MODEL), BF16),
            pltpu.VMEM((FFN, MODEL), BF16),
            pltpu.SemaphoreType.DMA((4,)),
            pltpu.SemaphoreType.DMA((16,)),
            pltpu.SemaphoreType.DMA((16,)),
        ],
        compiler_params=params(34),
        cost_estimate=cost(15),
    )(table, dgu, act, n, cot, *after)


def attention_back_kernel(table, *refs):
    a_in, h_in, cot_in = refs[:4], views(refs[4:8], 1), views(refs[8:12], 1)
    (r, gains), refs = refs[12:14], refs[14:]
    (q, k, v, o, cos, sin), (n_in, p_in), blocks, refs = refs[:6], refs[6:8], refs[8:13], refs[13:]
    x_in, refs = refs[:4], refs[4:]
    (r_one, *_), refs = refs[:1], refs[-27:]
    (dh_o, keep_o, send_o), outs, refs = refs[:3], refs[3:8], refs[8:]
    w, w_qkv, e, n, p, do, dq, dkv, dk, dv, made_out, made = refs[:12]
    w_sems, qkv_sems, out_sems, sems, load_sems, save_sems, chunk = refs[12:]
    qkv_copies = fetch(table, blocks, w_qkv, qkv_sems, 0)
    copies = fetch(table, blocks, w, w_sems, QKV)
    loads = [
        pltpu.make_async_copy(p_in, p, load_sems.at[0]),
        pltpu.make_async_copy(n_in, n, load_sems.at[1]),
    ]
    for load in loads:
        load.start()

    def joined(parts):
        return wide(jnp.concatenate([part[...] for part in parts], 1))

    scale = r[...]
    unit = joined(h_in) * scale
    a = joined(a_in) * wide(gains[1:2, :])
    d_h = joined(cot_in) + scale * (a - unit * jnp.mean(a * unit, -1, keepdims=True))
    dh_o[...] = d_h[:, :BLOCK]
    e[...] = narrow(d_h)
    wait(copies)
    do[...] = narrow(nt(w[...], e[...]))
    made_out[...] = narrow(nn(o[...], e[...]))
    scattered = scatter(table, made_out, outs, out_sems, QKV)

    loads[0].wait()
    dk[...] = jnp.zeros_like(dk)
    dv[...] = jnp.zeros_like(dv)
    for first in range(0, QROWS // HEAD, TOGETHER):
        for start in range(0, SEQ, QUERIES):
            stop = start + QUERIES
            queries = slice(start, stop)
            scores = []
            for h in range(first, first + TOGETHER):
                rows = slice(h * HEAD, (h + 1) * HEAD)
                probs = wide(p[h, :stop, queries])
                dp = tn(v[:, :stop], do[rows, queries])
                scores.append(narrow(probs * (dp - jnp.sum(probs * dp, 0, keepdims=True))))
            for h, ds in zip(range(first, first + TOGETHER), scores, strict=True):
                rows = slice(h * HEAD, (h + 1) * HEAD)
                d_q = nn(k[:, :stop], ds) * SCALE
                dq[rows, queries] = narrow(rotated_back(d_q, cos[:, queries], sin[:, queries]))
                dk[:, :stop] += nt(q[rows, queries], ds)
                dv[:, :stop] += nt(do[rows, queries], p[h, :stop, queries])
    dkv[:HEAD, :] = narrow(rotated_back(dk[...], cos[...], sin[...]))
    dkv[HEAD:, :] = narrow(dv[...])

    loads[1].wait()
    d = jnp.concatenate([dq[...], dkv[...]], 0)
    made[...] = narrow(nn(d, n[...]))
    scattered += scatter(table, made, outs, sems, 0)

    wait(qkv_copies)
    part = tn(d, w_qkv[...])
    product = narrow(part * (joined(x_in) * r_one[...] * wide(gains[0:1, :])))
    stat = narrow(nt(jnp.ones((16, MODEL), BF16), product))
    saved = []
    for k in range(4):
        chunk[k, :SEQ] = narrow(part[:, k * BLOCK : (k + 1) * BLOCK])
        chunk[k, SEQ:] = stat
        to = (keep_o, send_o)[k % 2].at[k // 2]
        saved.append(pltpu.make_async_copy(chunk.at[k], to, save_sems.at[k]))
        saved[-1].start()
    wait(saved)
    wait(scattered)


def attention_back(table, a, h, cot, r, gains, q, k, v, o, cos, sin, n, p, blocks, x, r_one, after):
    heads = QROWS // HEAD
    shapes = (out(SEQ, BLOCK, dtype=F32),)
    chunks = (out(2, SEQ + 16, BLOCK),) * 2
    return pl.pallas_call(
        attention_back_kernel,
        in_specs=[SCALARS]
        + whole(*a, *h, *cot, r, gains, q, k, v, o, cos, sin)
        + [ANYWHERE] * 7
        + whole(*x, r_one)
        + [ANYWHERE] * len(after),
        out_specs=(*whole(*shapes), *[ANYWHERE] * 7),
        out_shape=(*shapes, *chunks, *terms_shapes(GAINS_AT)),
        scratch_shapes=[
            pltpu.VMEM((QROWS, MODEL), BF16),
            pltpu.VMEM((QKV, MODEL), BF16),
            pltpu.VMEM((SEQ, MODEL), BF16),
            pltpu.VMEM((SEQ, MODEL), BF16),
            pltpu.VMEM((heads, SEQ, SEQ), BF16),
            pltpu.VMEM((QROWS, SEQ), BF16),
            pltpu.VMEM((QROWS, SEQ), BF16),
            pltpu.VMEM((2 * HEAD, SEQ), BF16),
            pltpu.VMEM((HEAD, SEQ), F32),
            pltpu.VMEM((HEAD, SEQ), F32),
            pltpu.VMEM((QROWS, MODEL), BF16),
            pltpu.VMEM((QKV, MODEL), BF16),
            pltpu.SemaphoreType.DMA((16,)),
            pltpu.SemaphoreType.DMA((16,)),
            pltpu.SemaphoreType.DMA((16,)),
            pltpu.SemaphoreType.DMA((16,)),
            pltpu.SemaphoreType.DMA((2,)),
            pltpu.SemaphoreType.DMA((4,)),
            pltpu.VMEM((4, SEQ + 16, BLOCK), BF16),
        ],
        compiler_params=params(34),
        cost_estimate=cost(22),
    )(table, *held_by((*a, *h, *cot)), r, gains, q, k, v, o, cos, sin, n, p, *blocks, *x, r_one, *after)


def outputs_kernel(h, m0, m1, m2, dh, c0, c1, x, r, gains, *refs):
    mixed_o, grad_o = refs[-2:]
    m = wide(m0[...]) + wide(m1[0]) + wide(m2[...])
    mixed_o[...] = narrow(to_natural(h[...] + m))
    total = wide(c0[...]) + wide(c1[...])
    stat = total[SEQ:].T[:, :1] * (1.0 / MODEL)
    scale = r[...]
    c_full = total[:SEQ] * wide(gains[0:1, :])
    grad_o[...] = to_natural(dh[...] + scale * (c_full - wide(x[...]) * scale * stat))


def outputs(h, m, dh, c, x, r, gains, after):
    shapes = (out(SEQ, BLOCK), out(SEQ, BLOCK, dtype=F32))
    args = (h, *m, dh, *c, x, r)
    return pl.pallas_call(
        outputs_kernel,
        grid=(1,),
        in_specs=whole(*args) + [spec((GAINS, BLOCK))] + [ANYWHERE] * len(after),
        out_specs=tuple(whole(*shapes)),
        out_shape=shapes,
        compiler_params=params(),
        cost_estimate=cost(5),
    )(*held_by(args), gains, *after)


def spread_eight(own, opposite, first, second):
    return own, cross(False)(first), cross(True)(second), swap_xh(opposite)


def gather_four(v):
    other = swap_xh(v)
    return v, swap_core(v), other, swap_core(other)


def gather_other(v):
    first, second = cross(False), cross(True)
    a, b = first(v), second(v)
    return (a, swap_core(a), b, swap_core(b)), second(a)


def gather_eight(v):
    a = cross(False)(v)
    both = cross(True)(bundle((v, a), ()))
    turned = swap_core(both)
    return (a, swap_core(a), (both, 0), (turned, 0)), (v, swap_core(v), (both, 1), (turned, 1))


def gather_own(v, opposite):
    return v, swap_core(v), opposite, swap_core(opposite)


def shards(
    tokens,
    w_query,
    key_value_weight,
    w_output,
    w_gate,
    w_up,
    w_down,
    gain_attention,
    gain_mlp,
    segment,
    position,
    cotangent,
):
    core = lax.axis_index("core")
    col = lax.axis_index("xh") * 2 + core
    upper = lax.axis_index("xl") == 1
    far, close = jnp.arange(4)[:, None], jnp.arange(4)[None, :]
    y = (lax.axis_index("y") ^ col) ^ jnp.where(core == 0, far, close)
    z = lax.axis_index("z") ^ jnp.where(core == 0, close, far)
    table = ((y * 4 + z) * 128).reshape(16).astype(jnp.int32)
    other_at = jnp.stack(
        [
            2 * BLOCK * core,
            BLOCK + 2 * BLOCK * (1 - core),
            2 * BLOCK * (1 - core),
            BLOCK + 2 * BLOCK * core,
            core,
            1 - core,
            lax.axis_index("xl"),
        ]
    ).astype(jnp.int32)

    x_own, cot_own, attn_rows = prepare(
        tokens, cotangent, w_query, key_value_weight, w_output.T, gain_attention, gain_mlp
    )
    mlp_keep, mlp_pack = prepare_mlp(other_at, w_gate, w_up, w_down.T)
    attn_shard = shard_attention(other_at, attn_rows, swap_xl(attn_rows), (mlp_pack,))
    x_all = gather_four(x_own)
    attn_blocks = gather_two(attn_shard, (mlp_pack,))
    mlp_shard = merge(
        other_at, mlp_keep, swap_xl(mlp_pack), (attn_blocks[1], attn_blocks[4])
    )
    cot_other, cot_self = gather_eight(cot_own)

    frequency = jnp.exp(jnp.arange(HALF).astype(F32) * (-2.0 * math.log(10000.0) / HEAD))
    angles = frequency[:, None] * position.astype(F32)[None, :]
    cos, sin = jnp.cos(angles), jnp.sin(angles)
    normed_one, probs, r_one, q, k, v, gains, o, keep, send = attention(
        table, x_all, cos, sin, segment[None, :], attn_blocks
    )
    here, there = add_cores(keep, send)
    resid = wide(x_own) + wide(here) + wide(swap_xh(there))
    resid_low = narrow(resid)
    mlp_blocks = gather_two(mlp_shard, (r_one,))
    h_other, opposite = gather_other(resid_low)
    h_self = gather_own(resid_low, opposite)
    r_two, n, cot, act, dgu, keep, send = mlp(
        table, other_at, (*h_other, *h_self), (*cot_other, *cot_self), gains, mlp_blocks
    )
    sums = add_cores(keep, send)
    mlp_terms = grads_mlp(table, dgu, act, n, cot, sums[:1])
    d_normed_two = sum_terms(spread_eight(sums[2], sums[3], sums[0], sums[1]))
    mlp_terms = tie(mlp_terms, d_normed_two)
    keep, send = down(table, other_at, act, mlp_blocks, (d_normed_two,))
    (opposite,) = tie((swap_xh(d_normed_two),), keep)
    keep, send = tie((keep, send), opposite)
    d_normed_all = gather_own(d_normed_two, opposite)
    mlp_terms = reduce_start(mlp_terms, ())
    away, second, own = add_cores_paired(keep, send)
    passed = cross(False)(away)
    mlp_out = own, (passed, 0), cross(True)(add_two(second, (passed, 1)))
    d_resid, keep, send, *attn_terms = attention_back(
        table,
        d_normed_all,
        h_self,
        cot_self,
        r_two,
        gains,
        q,
        k,
        v,
        o,
        cos,
        sin,
        normed_one,
        probs,
        attn_blocks,
        x_all,
        r_one,
        mlp_terms[:1],
    )
    here, there = add_cores(keep, send)

    d_normed_one = here, swap_xh(there)
    mlp_parts = reduce_end(*mlp_terms, ())
    attn_terms = reduce_start(attn_terms, (here, mlp_parts[0]))
    attn_parts = reduce_end(*attn_terms, d_normed_one[1:])
    mlp_total, mlp_pack = sum_pack(other_at, mlp_parts, attn_terms[:1])
    mixed, input_grad = outputs(
        resid, mlp_out, d_resid, d_normed_one, x_own, r_one, gains, attn_parts[:1]
    )
    attn_total, attn_pack = sum_pack(other_at, attn_parts, (mixed,))
    grad_gate, grad_up, grad_down, sum_two = finish_mlp(
        other_at, mlp_total, swap_xl(mlp_pack), w_gate, w_up
    )
    grad_query, grad_keyval, grad_output, sum_one = finish_attention(
        other_at, attn_total, swap_xl(attn_pack), w_query, key_value_weight
    )
    sums = jnp.concatenate([sum_one, sum_two], 0).reshape(1, 128)
    sums = (sums + swap_core(sums) + swap_xh(sums) + swap_both(sums)).reshape(2, 64)
    gain_one = sums[0] / wide(gain_attention)
    gain_two = sums[1] / wide(gain_mlp)
    return (
        mixed,
        input_grad,
        grad_query,
        grad_keyval,
        grad_output.T,
        grad_gate,
        grad_up,
        grad_down.T,
        gain_one,
        gain_two,
    )


def solution(mesh):
    fine = Mesh(mesh.devices.reshape(SIZES), AXES)
    both, turned, rows = P(ROW, COL), P(COL, ROW), P(ROW)
    return jax.shard_map(
        shards,
        mesh=fine,
        in_specs=(both, both, both, turned, both, both, turned, rows, rows, rows, rows, both),
        out_specs=(both, both, both, both, turned, both, both, turned, rows, rows),
        check_vma=False,
    )
```

```python
import functools
import math

import jax
import jax.numpy as jnp
from jax import lax
from jax.experimental import pallas as pl
from jax.experimental.pallas import tpu as pltpu
from jax.sharding import Mesh, PartitionSpec as P

F32, BF16 = jnp.float32, jnp.bfloat16
HEAD = 64
HALF = HEAD // 2
SCALE = 1.0 / math.sqrt(HEAD)
EPSILON = 1e-05
MASKED = -1e30
AXES = ("y", "xl", "z", "xh", "core")
SIZES = (4, 2, 4, 2, 2)
ROW, COL = ("y", "xl", "z"), ("xh", "core")

SEQ = 512
QUERIES = 256
TOGETHER = 4
MODEL = 2048
BLOCK = 512
QROWS = 512
QKV = QROWS + 128
GAINS_AT = QKV + 512
GAINS = 32
FFN = 704


def turn(second, mask):
    pairs = []
    for i in range(32):
        shift = 1 if (i % 2 == 0) != second else 3
        pairs.append((i, i ^ (mask << shift)))
    return lambda v: lax.ppermute(v, ("y", "z", "core"), pairs)


def cross(second):
    pairs = []
    for i in range(8):
        near = (i % 2 == 0) != second
        pairs.append((i, i ^ (4 if near else 6)))
    return lambda v: lax.ppermute(v, ("xl", "xh", "core"), pairs)


def swap_core(v):
    return lax.ppermute(v, "core", [(0, 1), (1, 0)])


def swap_xh(v):
    return lax.ppermute(v, "xh", [(0, 1), (1, 0)])


def swap_both(v):
    return lax.ppermute(v, ("xh", "core"), [(i, i ^ 3) for i in range(4)])


def swap_xl(v):
    return lax.ppermute(v, "xl", [(0, 1), (1, 0)])


def narrow(v):
    return v.astype(BF16)


def wide(v):
    return v.astype(F32)


def gather_two(v, after):
    held = bundle([v] + [turn(False, mask)(v) for mask in (1, 2, 3)], after)
    near, far = turn(True, 1), turn(True, 3)
    from_near, from_far = near(held), far(held)
    first, last = halves(from_near, from_far)
    return held, from_near, far(first), near(last), from_far


def reduce_start(terms, after):
    low, high, one, three, own = terms
    return (*add_halves(one, three, turn(True, 1)(low), turn(True, 3)(high), after), own)


def reduce_end(one, three, own, after):
    parts = sum_blocks(own, turn(True, 1)(one), turn(True, 3)(three), after)
    return [parts[0]] + [turn(False, mask)(parts[mask]) for mask in (1, 2, 3)]


def dot(a, b, contract):
    return lax.dot_general(a, b, ((contract[:1], contract[1:]), ((), ())), preferred_element_type=F32)


def nn(a, b):
    return dot(a, b, (1, 0))


def nt(a, b):
    return dot(a, b, (1, 1))


def tn(a, b):
    return dot(a, b, (0, 0))


def params(mib=14):
    return pltpu.CompilerParams(vmem_limit_bytes=mib * 1024 * 1024)


def cost(us):
    return pl.CostEstimate(flops=int(us * 1.15e9), bytes_accessed=0, transcendentals=0)


def spec(shape, index=None):
    zeros = (0,) * len(shape)
    return pl.BlockSpec(shape, index if index is not None else (lambda *_: zeros))


def held_by(arrays):
    return [a[0] if isinstance(a, tuple) else a for a in arrays]


def whole(*arrays):
    return [spec(a.shape) for a in held_by(arrays)]


def views(refs, k):
    return [ref.at[k] if len(ref.shape) == 3 else ref for ref in refs]


def out(*shape, dtype=BF16):
    return jax.ShapeDtypeStruct(shape, dtype)


def lane_low(shape):
    return lax.broadcasted_iota(jnp.int32, shape, 1) < 64


def pair(a, b):
    low = lane_low(a.shape)
    return jnp.where(low, a, pltpu.roll(b, 64, 1)), jnp.where(low, pltpu.roll(a, 64, 1), b)


def tie_kernel(*refs):
    pass


def tie(arrays, *after):
    count = len(arrays)
    return pl.pallas_call(
        tie_kernel,
        in_specs=[ANYWHERE] * (count + len(after)),
        out_specs=(ANYWHERE,) * count,
        out_shape=tuple(jax.ShapeDtypeStruct(v.shape, v.dtype) for v in arrays),
        input_output_aliases={k: k for k in range(count)},
        compiler_params=params(),
        cost_estimate=cost(1),
    )(*arrays, *after)


def inner(src, dst):
    t = [wide(src[:, k * 128 : (k + 1) * 128]) for k in range(4)]
    z0, z1 = pair(t[0], t[2])
    z2, z3 = pair(t[1], t[3])
    for k, value in enumerate((z0, z1, z2, z3)):
        dst[:, k * 128 : (k + 1) * 128] = narrow(value)


def column(row):
    n = row.shape[1]
    here = lax.broadcasted_iota(jnp.int32, (n, n), 0) == lax.broadcasted_iota(jnp.int32, (n, n), 1)
    return jnp.sum(jnp.where(here, wide(row[...]), 0.0), 1, keepdims=True)


def prepare_kernel(tokens, cot, w_q, w_kv, w_o, gain_a, gain_m, x_o, cot_o, rows_o):
    rows_o[:, :QROWS] = w_q[...]
    rows_o[:, QROWS:QKV] = w_kv[...]
    rows_o[:, QKV:GAINS_AT] = w_o[...]
    lane = lax.broadcasted_iota(jnp.int32, (64, GAINS), 1)
    gains = jnp.where(lane == 0, column(gain_a), jnp.where(lane == 1, column(gain_m), 0.0))
    rows_o[:, GAINS_AT:] = narrow(gains)
    inner(tokens, x_o)
    inner(cot, cot_o)


def prepare(tokens, cot, w_q, w_kv, w_o, gain_a, gain_m):
    shapes = (out(*tokens.shape), out(*cot.shape), out(64, GAINS_AT + GAINS))
    args = (tokens, cot, w_q, w_kv, w_o, gain_a[None, :], gain_m[None, :])
    return pl.pallas_call(
        prepare_kernel,
        in_specs=whole(*args),
        out_specs=tuple(whole(*shapes)),
        out_shape=shapes,
        compiler_params=params(),
        cost_estimate=cost(3),
    )(*args)


def shard_attention_kernel(where, mine, other, *refs):
    upper = where[6] == 1
    a, b = wide(mine[...]), wide(other[...])
    rows = jnp.concatenate([jnp.where(upper, b, a), jnp.where(upper, a, b)], 0)
    refs[-1][...] = narrow(rows.T)


def shard_attention(where, mine, other, after):
    shape = out(mine.shape[1], 128)
    return pl.pallas_call(
        shard_attention_kernel,
        in_specs=[SCALARS] + whole(mine, other) + [ANYWHERE] * len(after),
        out_specs=spec(shape.shape),
        out_shape=shape,
        compiler_params=params(),
        cost_estimate=cost(2),
    )(where, mine, other, *after)


def prepare_mlp_kernel(where, w_g, w_u, w_d, keep_o, pack_o, held):
    for k, w in enumerate((w_g, w_u, w_d)):
        value = wide(w[...])
        both = jnp.concatenate([value[:, :FFN], value[:, FFN:]], 0)
        held[k * FFN : (k + 1) * FFN] = both.T
    keep_o[...] = narrow(held[...])
    pack_o[...] = narrow(packed(held[...], where[6] == 1))


def prepare_mlp(where, w_g, w_u, w_d):
    rows = 3 * FFN
    shapes = (out(rows, 128), out(rows // 2, 128))
    return pl.pallas_call(
        prepare_mlp_kernel,
        in_specs=[SCALARS] + whole(w_g, w_u, w_d),
        out_specs=tuple(whole(*shapes)),
        out_shape=shapes,
        scratch_shapes=[pltpu.VMEM((rows, 128), F32)],
        compiler_params=params(),
        cost_estimate=cost(4),
    )(where, w_g, w_u, w_d)


def sum_terms_kernel(a, b, c, d, total_o):
    total_o[...] = narrow(wide(a[...]) + wide(b[...]) + wide(c[...]) + wide(d[...]))


def sum_terms(terms):
    shape = out(*terms[0].shape)
    return pl.pallas_call(
        sum_terms_kernel,
        in_specs=whole(*terms),
        out_specs=spec(shape.shape),
        out_shape=shape,
        compiler_params=params(),
        cost_estimate=cost(2),
    )(*terms)


def add_split_kernel(a, b, *outs):
    for k, ref in enumerate(outs):
        ref[...] = narrow(wide(a[k]) + wide(b[k]))


def add_cores(keep, send):
    shapes = (out(*keep.shape[1:]),) * keep.shape[0]
    return pl.pallas_call(
        add_split_kernel,
        in_specs=whole(keep, send),
        out_specs=tuple(whole(*shapes)),
        out_shape=shapes,
        compiler_params=params(),
        cost_estimate=cost(2),
    )(keep, swap_core(send))


def add_two_kernel(a, b, total_o):
    total_o[...] = narrow(wide(a[...]) + wide(b[1]))


def add_two(a, b):
    return pl.pallas_call(
        add_two_kernel,
        in_specs=whole(a, b),
        out_specs=spec(a.shape),
        out_shape=out(*a.shape),
        compiler_params=params(),
        cost_estimate=cost(1),
    )(*held_by((a, b)))


def add_paired_kernel(a, b, pair_o, second_o, own_o):
    total = lambda k: narrow(wide(a[k]) + wide(b[k]))
    pair_o[0] = total(0)
    second_o[...] = total(1)
    own_o[...] = total(2)
    pair_o[1] = total(3)


def add_cores_paired(keep, send):
    block = out(*keep.shape[1:])
    shapes = (out(2, *keep.shape[1:]), block, block)
    return pl.pallas_call(
        add_paired_kernel,
        in_specs=whole(keep, send),
        out_specs=tuple(whole(*shapes)),
        out_shape=shapes,
        compiler_params=params(),
        cost_estimate=cost(3),
    )(keep, swap_core(send))


def to_natural(v):
    z = [v[:, k * 128 : (k + 1) * 128] for k in range(4)]
    t0, t2 = pair(z[0], z[1])
    t1, t3 = pair(z[2], z[3])
    return jnp.concatenate([t0, t1, t2, t3], 1)


def fetch(table, blocks, target, sems, start):
    rows = target.shape[0]
    copies = []
    for j in range(4):
        for i in range(4):
            src = block_of(blocks, j, i)
            lanes = pl.multiple_of(table[4 * j + i], 128)
            copy = pltpu.make_async_copy(
                src.at[pl.ds(start, rows)], target.at[:, pl.ds(lanes, 128)], sems.at[len(copies)]
            )
            copy.start()
            copies.append(copy)
    return copies


def block_of(blocks, j, i):
    own, one, low, high, three = blocks
    if j == 2:
        return low.at[i] if i < 2 else high.at[i - 2]
    return (own, one, None, three)[j].at[i]


def wait(copies):
    for copy in copies:
        copy.wait()


ANYWHERE = pl.BlockSpec(memory_space=pl.ANY)
SCALARS = pl.BlockSpec(memory_space=pltpu.SMEM)


def halves_kernel(a, b, a_o, b_o):
    a_o[...] = a[...]
    b_o[...] = b[...]


def halves(a, b):
    block = (2,) + a.shape[1:]
    first = spec(block, lambda i: (0, 0, 0))
    return pl.pallas_call(
        halves_kernel,
        grid=(1,),
        in_specs=[first, spec(block, lambda i: (1, 0, 0))],
        out_specs=(first, first),
        out_shape=(out(*block),) * 2,
        compiler_params=params(),
        cost_estimate=cost(2),
    )(a, b)


def add_halves_kernel(one, three, low, high, *refs):
    one_o, three_o = refs[-2:]
    three_o[...] = narrow(wide(three[...]) + wide(low[...]))
    one_o[...] = narrow(wide(one[...]) + wide(high[...]))


def add_halves(one, three, low, high, after):
    block = (1,) + one.shape[1:]
    first, last = spec(block, lambda i: (i, 0, 0)), spec(block, lambda i: (2 + i, 0, 0))
    return pl.pallas_call(
        add_halves_kernel,
        grid=(2,),
        in_specs=[last, first, first, first] + [ANYWHERE] * len(after),
        out_specs=(last, first),
        out_shape=(out(*one.shape),) * 2,
        input_output_aliases={0: 0, 1: 1},
        compiler_params=params(),
        cost_estimate=cost(2),
    )(one, three, low, high, *after)


def sum_blocks_kernel(a, b, c, *refs):
    for k, ref in enumerate(refs[-4:]):
        ref[...] = narrow(wide(a[k]) + wide(b[k]) + wide(c[k]))


def sum_blocks(a, b, c, after):
    shapes = (out(*a.shape[1:]),) * 4
    return pl.pallas_call(
        sum_blocks_kernel,
        in_specs=whole(a, b, c) + [ANYWHERE] * len(after),
        out_specs=tuple(whole(*shapes)),
        out_shape=shapes,
        compiler_params=params(),
        cost_estimate=cost(3),
    )(a, b, c, *after)


def packed(v, upper):
    half = v.shape[0] // 2
    top, bottom = v[:half], v[half:]
    low = lane_low(top.shape)
    return jnp.where(
        upper,
        jnp.where(low, top, pltpu.roll(bottom, 64, 1)),
        jnp.where(low, pltpu.roll(top, 64, 1), bottom),
    )


def unpacked(v, upper):
    turned = pltpu.roll(v, 64, 1)
    return [jnp.where(upper, v, turned), jnp.where(upper, turned, v)]


def own_lanes(shape, upper):
    return lane_low(shape) != upper


def sum_pack_kernel(where, *refs, count):
    sum_o, pack_o = refs[-2:]
    total = wide(refs[0][...])
    for ref in refs[1:count]:
        total += wide(ref[...])
    sum_o[...] = total
    pack_o[...] = narrow(packed(total, where[6] == 1))


def sum_pack(where, parts, after):
    rows = parts[0].shape[0]
    shapes = (out(rows, 128, dtype=F32), out(rows // 2, 128))
    return pl.pallas_call(
        functools.partial(sum_pack_kernel, count=len(parts)),
        in_specs=[SCALARS] + whole(*parts) + [ANYWHERE] * len(after),
        out_specs=tuple(whole(*shapes)),
        out_shape=shapes,
        compiler_params=params(),
        cost_estimate=cost(2),
    )(where, *parts, *after)


def merge_kernel(where, keep, other, *refs):
    upper = where[6] == 1
    half = other.shape[0]
    for k, part in enumerate(unpacked(wide(other[...]), upper)):
        rows = slice(k * half, (k + 1) * half)
        refs[-1][rows] = narrow(
            jnp.where(own_lanes(part.shape, upper), wide(keep[rows, :]), part)
        )


def merge(where, keep, other, after):
    return pl.pallas_call(
        merge_kernel,
        in_specs=[SCALARS] + whole(keep, other) + [ANYWHERE] * len(after),
        out_specs=spec(keep.shape),
        out_shape=out(*keep.shape),
        compiler_params=params(),
        cost_estimate=cost(2),
    )(where, keep, other, *after)


def row_dot(weight, grad):
    return jnp.sum(wide(weight) * grad, -1, keepdims=True)


def finish_mlp_kernel(where, total, other, w_gate, w_up, gate_o, up_o, down_o, sum_o, held):
    upper = where[6] == 1
    half = other.shape[0]
    for k, part in enumerate(unpacked(wide(other[...]), upper)):
        rows = slice(k * half, (k + 1) * half)
        held[rows] = jnp.where(own_lanes(part.shape, upper), total[rows, :], part)
    for k, ref in enumerate((gate_o, up_o, down_o)):
        turned = held[k * FFN : (k + 1) * FFN].T
        ref[:, :FFN] = turned[:64]
        ref[:, FFN:] = turned[64:]
    sum_o[...] = row_dot(w_gate[...], gate_o[...]) + row_dot(w_up[...], up_o[...])


def finish_mlp(where, total, other, w_gate, w_up):
    shapes = (out(64, 2 * FFN, dtype=F32),) * 3 + (out(64, 1, dtype=F32),)
    return pl.pallas_call(
        finish_mlp_kernel,
        in_specs=[SCALARS] + whole(total, other, w_gate, w_up),
        out_specs=tuple(whole(*shapes)),
        out_shape=shapes,
        scratch_shapes=[pltpu.VMEM(total.shape, F32)],
        compiler_params=params(),
        cost_estimate=cost(4),
    )(where, total, other, w_gate, w_up)


def finish_attention_kernel(where, total, other, w_q, w_kv, q_o, kv_o, out_o, sum_o, held):
    upper = where[6] == 1
    half = other.shape[0]
    for k, part in enumerate(unpacked(wide(other[...]), upper)):
        rows = slice(k * half, (k + 1) * half)
        held[:, rows] = (total[rows, :] + pltpu.roll(part, 64, 1)).T
    mine = held[pl.ds(pl.multiple_of(where[6] * 64, 64), 64), :]
    q_o[...] = mine[:, :QROWS]
    kv_o[...] = mine[:, QROWS:QKV]
    out_o[...] = mine[:, QKV:]
    sum_o[...] = row_dot(w_q[...], q_o[...]) + row_dot(w_kv[...], kv_o[...])


def finish_attention(where, total, other, w_q, w_kv):
    shapes = tuple(out(64, n, dtype=F32) for n in (QROWS, QKV - QROWS, QROWS, 1))
    return pl.pallas_call(
        finish_attention_kernel,
        in_specs=[SCALARS] + whole(total, other, w_q, w_kv),
        out_specs=tuple(whole(*shapes)),
        out_shape=shapes,
        scratch_shapes=[pltpu.VMEM((128, total.shape[0]), F32)],
        compiler_params=params(),
        cost_estimate=cost(3),
    )(where, total, other, w_q, w_kv)


def rotated(v, cos, sin):
    a, b = v[:HALF], v[HALF:]
    return jnp.concatenate([a * cos - b * sin, b * cos + a * sin], 0)


def rotated_back(v, cos, sin):
    a, b = v[:HALF], v[HALF:]
    return jnp.concatenate([a * cos + b * sin, b * cos - a * sin], 0)


def bundle_kernel(*refs, count):
    for k in range(count):
        refs[-1][k] = refs[k][...]


def bundle(parts, after):
    shape = out(len(parts), *parts[0].shape)
    return pl.pallas_call(
        functools.partial(bundle_kernel, count=len(parts)),
        in_specs=whole(*parts) + [ANYWHERE] * len(after),
        out_specs=spec(shape.shape),
        out_shape=shape,
        compiler_params=params(),
        cost_estimate=cost(2),
    )(*parts, *after)


def attention_kernel(table, x0, x1, x2, x3, cos, sin, segment, *refs):
    blocks, refs = refs[:5], refs[-20:]
    n_o, p_o, r_o, q_o, k_o, v_o, gains_o, o_o, keep_o, send_o = refs[:10]
    w, w_out, n, probs, bias, w_sems, out_sems, gain_sems, n_sem, p_sems = refs[10:]
    copies = fetch(table, blocks, gains_o, gain_sems, GAINS_AT)
    w_copies = fetch(table, blocks, w, w_sems, 0)
    out_copies = fetch(table, blocks, w_out, out_sems, QKV)
    x = wide(jnp.concatenate([x0[...], x1[...], x2[...], x3[...]], 1))
    r = lax.rsqrt(jnp.mean(x * x, -1, keepdims=True) + EPSILON)
    r_o[...] = r
    wait(copies)
    n[...] = narrow(x * r * wide(gains_o[0:1, :]))
    saved = [pltpu.make_async_copy(n, n_o, n_sem)]
    saved[0].start()

    shape = (SEQ, SEQ)
    key = lax.broadcasted_iota(jnp.int32, shape, 0)
    query = lax.broadcasted_iota(jnp.int32, shape, 1)
    allowed = (column(segment) == wide(segment[...])) & (key <= query)
    bias[...] = jnp.where(allowed, 0.0, MASKED)

    wait(w_copies)
    qkv = nt(w[...], n[...])
    c, s = cos[...], sin[...]
    for h in range(QROWS // HEAD):
        head = rotated(qkv[h * HEAD : (h + 1) * HEAD], c, s)
        q_o[h * HEAD : (h + 1) * HEAD, :] = narrow(head) * SCALE
    k_o[...] = narrow(rotated(qkv[QROWS : QROWS + HEAD], c, s))
    v_o[...] = narrow(qkv[QROWS + HEAD :])

    for first in range(0, QROWS // HEAD, TOGETHER):
        for start in range(0, SEQ, QUERIES):
            stop = start + QUERIES
            queries = slice(start, stop)
            for h in range(first, first + TOGETHER):
                rows = slice(h * HEAD, (h + 1) * HEAD)
                s = tn(k_o[:, :stop], q_o[rows, queries]) + bias[:stop, queries]
                e = jnp.exp(s - jnp.max(s, 0, keepdims=True))
                probs[h, :stop, queries] = narrow(e * (1.0 / jnp.sum(e, 0, keepdims=True)))
            for h in range(first, first + TOGETHER):
                rows = slice(h * HEAD, (h + 1) * HEAD)
                o_o[rows, queries] = narrow(nn(v_o[:, :stop], probs[h, :stop, queries]))
        some = pl.ds(first, TOGETHER)
        saved.append(pltpu.make_async_copy(probs.at[some], p_o.at[some], p_sems.at[first]))
        saved[-1].start()

    wait(out_copies)
    value = tn(o_o[...], w_out[...])
    for k in range(4):
        (keep_o, send_o)[k % 2][k // 2] = narrow(value[:, k * BLOCK : (k + 1) * BLOCK])
    wait(saved)


def attention(table, x, cos, sin, segment, blocks):
    heads = QROWS // HEAD
    shapes = (
        out(SEQ, 1, dtype=F32),
        out(QROWS, SEQ),
        out(HEAD, SEQ),
        out(HEAD, SEQ),
        out(GAINS, MODEL),
        out(QROWS, SEQ),
        out(2, SEQ, BLOCK),
        out(2, SEQ, BLOCK),
    )
    return pl.pallas_call(
        attention_kernel,
        in_specs=[SCALARS]
        + whole(*x, cos, sin, segment)
        + [ANYWHERE] * 5,
        out_specs=(ANYWHERE, ANYWHERE, *whole(*shapes)),
        out_shape=(out(SEQ, MODEL), out(heads, SEQ, SEQ), *shapes),
        scratch_shapes=[
            pltpu.VMEM((QKV, MODEL), BF16),
            pltpu.VMEM((QROWS, MODEL), BF16),
            pltpu.VMEM((SEQ, MODEL), BF16),
            pltpu.VMEM((heads, SEQ, SEQ), BF16),
            pltpu.VMEM((SEQ, SEQ), F32),
            pltpu.SemaphoreType.DMA((16,)),
            pltpu.SemaphoreType.DMA((16,)),
            pltpu.SemaphoreType.DMA((16,)),
            pltpu.SemaphoreType.DMA,
            pltpu.SemaphoreType.DMA((heads,)),
        ],
        compiler_params=params(28),
        cost_estimate=cost(14),
    )(table, *x, cos, sin, segment, *blocks)


def mlp_kernel(table, where, *refs):
    h_in, cot_in = (views(refs[k : k + 4], 0) + views(refs[k + 4 : k + 8], 1) for k in (0, 8))
    gains, blocks, refs = refs[16], refs[17:22], refs[22:]
    r_o, n_o, cot_o, act_o, dgu_o, keep_o, send_o = refs[:7]
    w, wd, h, cot, n, act, dgu, chunk, sems, wd_sems, saves = refs[7:]
    copies = fetch(table, blocks, w, sems, 0)
    wd_copies = fetch(table, blocks, wd, wd_sems, 2 * FFN)
    saved = []

    def save(src, dst):
        copy = pltpu.make_async_copy(src, dst, saves.at[len(saved)])
        copy.start()
        saved.append(copy)

    for part in range(2):
        tokens = pl.ds(part * SEQ, SEQ)
        for k in range(4):
            lanes = slice(k * BLOCK, (k + 1) * BLOCK)
            if part == 0:
                lanes = pl.ds(pl.multiple_of(where[k], BLOCK), BLOCK)
            h[:, lanes] = h_in[4 * part + k][...]
            cot[part, :, lanes] = cot_in[4 * part + k][...]
        save(cot.at[part], cot_o.at[tokens])
        hidden = wide(h[...])
        r = lax.rsqrt(jnp.mean(hidden * hidden, -1, keepdims=True) + EPSILON)
        r_o[...] = r
        n[part] = narrow(hidden * r * wide(gains[1:2, :]))
        save(n.at[part], n_o.at[tokens])

    wait(copies)
    wait(wd_copies)
    for part in range(2):
        tokens = pl.ds(part * SEQ, SEQ)
        both = nt(w[...], n[part])
        d_out = nt(wd[...], cot[part])
        gate, up = both[:FFN], both[FFN:]
        g = jax.nn.sigmoid(gate)
        silu = gate * g
        act[part] = narrow(silu * up)
        save(act.at[part], act_o.at[:, tokens])
        dgu[part, :FFN] = narrow(d_out * up * (g + silu * (1.0 - g)))
        dgu[part, FFN:] = narrow(d_out * silu)
        save(dgu.at[part], dgu_o.at[:, tokens])
        d_n = tn(dgu[part], w[...])
        for k in range(4):
            chunk[4 * part + k] = narrow(d_n[:, k * BLOCK : (k + 1) * BLOCK])
            block = 2 + k // 2 if part else where[4 + k % 2] ^ (k // 2)
            save(chunk.at[4 * part + k], (keep_o, send_o)[k % 2].at[block])
    wait(saved)


def mlp(table, where, h, cot, gains, blocks):
    shapes = (
        out(2 * SEQ, MODEL),
        out(2 * SEQ, MODEL),
        out(FFN, 2 * SEQ),
        out(2 * FFN, 2 * SEQ),
        out(4, SEQ, BLOCK),
        out(4, SEQ, BLOCK),
    )
    return pl.pallas_call(
        mlp_kernel,
        in_specs=[SCALARS] * 2 + whole(*h, *cot, gains) + [ANYWHERE] * 5,
        out_specs=(spec((SEQ, 1)),) + (ANYWHERE,) * 6,
        out_shape=(out(SEQ, 1, dtype=F32), *shapes),
        scratch_shapes=[
            pltpu.VMEM((2 * FFN, MODEL), BF16),
            pltpu.VMEM((FFN, MODEL), BF16),
            pltpu.VMEM((SEQ, MODEL), BF16),
            pltpu.VMEM((2, SEQ, MODEL), BF16),
            pltpu.VMEM((2, SEQ, MODEL), BF16),
            pltpu.VMEM((2, FFN, SEQ), BF16),
            pltpu.VMEM((2, 2 * FFN, SEQ), BF16),
            pltpu.VMEM((8, SEQ, BLOCK), BF16),
            pltpu.SemaphoreType.DMA((16,)),
            pltpu.SemaphoreType.DMA((16,)),
            pltpu.SemaphoreType.DMA((16,)),
        ],
        compiler_params=params(42),
        cost_estimate=cost(30),
    )(table, where, *held_by((*h, *cot)), gains, *blocks)


def down_kernel(table, where, act, *refs):
    blocks, (keep_o, send_o, w, sems) = refs[:5], refs[-4:]
    wait(fetch(table, blocks, w, sems, 2 * FFN))
    value = tn(act[...], w[...])
    for k in range(4):
        lanes = slice(k * BLOCK, (k + 1) * BLOCK)
        to = (keep_o, send_o)[k % 2]
        to[where[4 + k % 2] ^ (k // 2)] = narrow(value[:SEQ, lanes])
        to[2 + k // 2] = narrow(value[SEQ:, lanes])


def down(table, where, act, blocks, after):
    shapes = (out(4, SEQ, BLOCK),) * 2
    return pl.pallas_call(
        down_kernel,
        in_specs=[SCALARS] * 2 + whole(act) + [ANYWHERE] * (5 + len(after)),
        out_specs=tuple(whole(*shapes)),
        out_shape=shapes,
        scratch_shapes=[pltpu.VMEM((FFN, MODEL), BF16), pltpu.SemaphoreType.DMA((16,))],
        compiler_params=params(20),
        cost_estimate=cost(7),
    )(table, where, act, *blocks, *after)


def scatter(table, source, outs, sems, row):
    rows = source.shape[0]
    low, high, one, three, own = outs
    blocks = own, one, low, high, three
    copies = []
    for j in range(4):
        for i in range(4):
            lanes = pl.multiple_of(table[4 * j + i], 128)
            copy = pltpu.make_async_copy(
                source.at[:, pl.ds(lanes, 128)],
                block_of(blocks, j, i).at[pl.ds(row, rows)],
                sems.at[len(copies)],
            )
            copy.start()
            copies.append(copy)
    return copies


def terms_shapes(rows):
    return (out(2, rows, 128),) * 2 + (out(4, rows, 128),) * 3


def grads_mlp_kernel(table, dgu_in, act_in, n_in, cot_in, *refs):
    outs, (dgu, act, n, cot, made, made_down, load_sems, sems, down_sems) = refs[-14:-9], refs[-9:]
    loads = [
        pltpu.make_async_copy(src, dst, load_sems.at[k])
        for k, (src, dst) in enumerate(((dgu_in, dgu), (n_in, n), (act_in, act), (cot_in, cot)))
    ]
    for load in loads:
        load.start()
    wait(loads[:2])
    made[...] = narrow(nn(dgu[...], n[...]))
    copies = scatter(table, made, outs, sems, 0)
    wait(loads[2:])
    made_down[...] = narrow(nn(act[...], cot[...]))
    copies += scatter(table, made_down, outs, down_sems, 2 * FFN)
    wait(copies)


def grads_mlp(table, dgu, act, n, cot, after):
    shapes = terms_shapes(3 * FFN)
    return pl.pallas_call(
        grads_mlp_kernel,
        in_specs=[SCALARS] + [ANYWHERE] * (4 + len(after)),
        out_specs=(ANYWHERE,) * len(shapes),
        out_shape=shapes,
        scratch_shapes=[
            pltpu.VMEM(dgu.shape, BF16),
            pltpu.VMEM(act.shape, BF16),
            pltpu.VMEM(n.shape, BF16),
            pltpu.VMEM(cot.shape, BF16),
            pltpu.VMEM((2 * FFN, MODEL), BF16),
            pltpu.VMEM((FFN, MODEL), BF16),
            pltpu.SemaphoreType.DMA((4,)),
            pltpu.SemaphoreType.DMA((16,)),
            pltpu.SemaphoreType.DMA((16,)),
        ],
        compiler_params=params(34),
        cost_estimate=cost(15),
    )(table, dgu, act, n, cot, *after)


def attention_back_kernel(table, *refs):
    a_in, h_in, cot_in = refs[:4], views(refs[4:8], 1), views(refs[8:12], 1)
    (r, gains), refs = refs[12:14], refs[14:]
    (q, k, v, o, cos, sin), (n_in, p_in), blocks, refs = refs[:6], refs[6:8], refs[8:13], refs[13:]
    x_in, refs = refs[:4], refs[4:]
    (r_one, *_), refs = refs[:1], refs[-27:]
    (dh_o, keep_o, send_o), outs, refs = refs[:3], refs[3:8], refs[8:]
    w, w_qkv, e, n, p, do, dq, dkv, dk, dv, made_out, made = refs[:12]
    w_sems, qkv_sems, out_sems, sems, load_sems, save_sems, chunk = refs[12:]
    qkv_copies = fetch(table, blocks, w_qkv, qkv_sems, 0)
    copies = fetch(table, blocks, w, w_sems, QKV)
    loads = [
        pltpu.make_async_copy(p_in, p, load_sems.at[0]),
        pltpu.make_async_copy(n_in, n, load_sems.at[1]),
    ]
    for load in loads:
        load.start()

    def joined(parts):
        return wide(jnp.concatenate([part[...] for part in parts], 1))

    scale = r[...]
    unit = joined(h_in) * scale
    a = joined(a_in) * wide(gains[1:2, :])
    d_h = joined(cot_in) + scale * (a - unit * jnp.mean(a * unit, -1, keepdims=True))
    dh_o[...] = d_h[:, :BLOCK]
    e[...] = narrow(d_h)
    wait(copies)
    do[...] = narrow(nt(w[...], e[...]))
    made_out[...] = narrow(nn(o[...], e[...]))
    scattered = scatter(table, made_out, outs, out_sems, QKV)

    loads[0].wait()
    dk[...] = jnp.zeros_like(dk)
    dv[...] = jnp.zeros_like(dv)
    for first in range(0, QROWS // HEAD, TOGETHER):
        for start in range(0, SEQ, QUERIES):
            stop = start + QUERIES
            queries = slice(start, stop)
            scores = []
            for h in range(first, first + TOGETHER):
                rows = slice(h * HEAD, (h + 1) * HEAD)
                probs = wide(p[h, :stop, queries])
                dp = tn(v[:, :stop], do[rows, queries])
                scores.append(narrow(probs * (dp - jnp.sum(probs * dp, 0, keepdims=True))))
            for h, ds in zip(range(first, first + TOGETHER), scores, strict=True):
                rows = slice(h * HEAD, (h + 1) * HEAD)
                d_q = nn(k[:, :stop], ds) * SCALE
                dq[rows, queries] = narrow(rotated_back(d_q, cos[:, queries], sin[:, queries]))
                dk[:, :stop] += nt(q[rows, queries], ds)
                dv[:, :stop] += nt(do[rows, queries], p[h, :stop, queries])
    dkv[:HEAD, :] = narrow(rotated_back(dk[...], cos[...], sin[...]))
    dkv[HEAD:, :] = narrow(dv[...])

    loads[1].wait()
    d = jnp.concatenate([dq[...], dkv[...]], 0)
    made[...] = narrow(nn(d, n[...]))
    scattered += scatter(table, made, outs, sems, 0)

    wait(qkv_copies)
    part = tn(d, w_qkv[...])
    product = narrow(part * (joined(x_in) * r_one[...] * wide(gains[0:1, :])))
    stat = narrow(nt(jnp.ones((16, MODEL), BF16), product))
    saved = []
    for k in range(4):
        chunk[k, :SEQ] = narrow(part[:, k * BLOCK : (k + 1) * BLOCK])
        chunk[k, SEQ:] = stat
        to = (keep_o, send_o)[k % 2].at[k // 2]
        saved.append(pltpu.make_async_copy(chunk.at[k], to, save_sems.at[k]))
        saved[-1].start()
    wait(saved)
    wait(scattered)


def attention_back(table, a, h, cot, r, gains, q, k, v, o, cos, sin, n, p, blocks, x, r_one, after):
    heads = QROWS // HEAD
    shapes = (out(SEQ, BLOCK, dtype=F32),)
    chunks = (out(2, SEQ + 16, BLOCK),) * 2
    return pl.pallas_call(
        attention_back_kernel,
        in_specs=[SCALARS]
        + whole(*a, *h, *cot, r, gains, q, k, v, o, cos, sin)
        + [ANYWHERE] * 7
        + whole(*x, r_one)
        + [ANYWHERE] * len(after),
        out_specs=(*whole(*shapes), *[ANYWHERE] * 7),
        out_shape=(*shapes, *chunks, *terms_shapes(GAINS_AT)),
        scratch_shapes=[
            pltpu.VMEM((QROWS, MODEL), BF16),
            pltpu.VMEM((QKV, MODEL), BF16),
            pltpu.VMEM((SEQ, MODEL), BF16),
            pltpu.VMEM((SEQ, MODEL), BF16),
            pltpu.VMEM((heads, SEQ, SEQ), BF16),
            pltpu.VMEM((QROWS, SEQ), BF16),
            pltpu.VMEM((QROWS, SEQ), BF16),
            pltpu.VMEM((2 * HEAD, SEQ), BF16),
            pltpu.VMEM((HEAD, SEQ), F32),
            pltpu.VMEM((HEAD, SEQ), F32),
            pltpu.VMEM((QROWS, MODEL), BF16),
            pltpu.VMEM((QKV, MODEL), BF16),
            pltpu.SemaphoreType.DMA((16,)),
            pltpu.SemaphoreType.DMA((16,)),
            pltpu.SemaphoreType.DMA((16,)),
            pltpu.SemaphoreType.DMA((16,)),
            pltpu.SemaphoreType.DMA((2,)),
            pltpu.SemaphoreType.DMA((4,)),
            pltpu.VMEM((4, SEQ + 16, BLOCK), BF16),
        ],
        compiler_params=params(34),
        cost_estimate=cost(22),
    )(table, *held_by((*a, *h, *cot)), r, gains, q, k, v, o, cos, sin, n, p, *blocks, *x, r_one, *after)


def outputs_kernel(h, m0, m1, m2, dh, c0, c1, x, r, gains, *refs):
    mixed_o, grad_o = refs[-2:]
    m = wide(m0[...]) + wide(m1[0]) + wide(m2[...])
    mixed_o[...] = narrow(to_natural(h[...] + m))
    total = wide(c0[...]) + wide(c1[...])
    stat = total[SEQ:].T[:, :1] * (1.0 / MODEL)
    scale = r[...]
    c_full = total[:SEQ] * wide(gains[0:1, :])
    grad_o[...] = to_natural(dh[...] + scale * (c_full - wide(x[...]) * scale * stat))


def outputs(h, m, dh, c, x, r, gains, after):
    shapes = (out(SEQ, BLOCK), out(SEQ, BLOCK, dtype=F32))
    args = (h, *m, dh, *c, x, r)
    return pl.pallas_call(
        outputs_kernel,
        grid=(1,),
        in_specs=whole(*args) + [spec((GAINS, BLOCK))] + [ANYWHERE] * len(after),
        out_specs=tuple(whole(*shapes)),
        out_shape=shapes,
        compiler_params=params(),
        cost_estimate=cost(5),
    )(*held_by(args), gains, *after)


def spread_eight(own, opposite, first, second):
    return own, cross(False)(first), cross(True)(second), swap_xh(opposite)


def gather_four(v):
    other = swap_xh(v)
    return v, swap_core(v), other, swap_core(other)


def gather_other(v):
    first, second = cross(False), cross(True)
    a, b = first(v), second(v)
    return (a, swap_core(a), b, swap_core(b)), second(a)


def gather_eight(v):
    a = cross(False)(v)
    both = cross(True)(bundle((v, a), ()))
    turned = swap_core(both)
    return (a, swap_core(a), (both, 0), (turned, 0)), (v, swap_core(v), (both, 1), (turned, 1))


def gather_own(v, opposite):
    return v, swap_core(v), opposite, swap_core(opposite)


def shards(
    tokens,
    w_query,
    key_value_weight,
    w_output,
    w_gate,
    w_up,
    w_down,
    gain_attention,
    gain_mlp,
    segment,
    position,
    cotangent,
):
    core = lax.axis_index("core")
    col = lax.axis_index("xh") * 2 + core
    upper = lax.axis_index("xl") == 1
    far, close = jnp.arange(4)[:, None], jnp.arange(4)[None, :]
    y = (lax.axis_index("y") ^ col) ^ jnp.where(core == 0, far, close)
    z = lax.axis_index("z") ^ jnp.where(core == 0, close, far)
    table = ((y * 4 + z) * 128).reshape(16).astype(jnp.int32)
    other_at = jnp.stack(
        [
            2 * BLOCK * core,
            BLOCK + 2 * BLOCK * (1 - core),
            2 * BLOCK * (1 - core),
            BLOCK + 2 * BLOCK * core,
            core,
            1 - core,
            lax.axis_index("xl"),
        ]
    ).astype(jnp.int32)

    x_own, cot_own, attn_rows = prepare(
        tokens, cotangent, w_query, key_value_weight, w_output.T, gain_attention, gain_mlp
    )
    mlp_keep, mlp_pack = prepare_mlp(other_at, w_gate, w_up, w_down.T)
    attn_shard = shard_attention(other_at, attn_rows, swap_xl(attn_rows), (mlp_pack,))
    x_all = gather_four(x_own)
    attn_blocks = gather_two(attn_shard, (mlp_pack,))
    mlp_shard = merge(
        other_at, mlp_keep, swap_xl(mlp_pack), (attn_blocks[1], attn_blocks[4])
    )
    cot_other, cot_self = gather_eight(cot_own)

    frequency = jnp.exp(jnp.arange(HALF).astype(F32) * (-2.0 * math.log(10000.0) / HEAD))
    angles = frequency[:, None] * position.astype(F32)[None, :]
    cos, sin = jnp.cos(angles), jnp.sin(angles)
    normed_one, probs, r_one, q, k, v, gains, o, keep, send = attention(
        table, x_all, cos, sin, segment[None, :], attn_blocks
    )
    here, there = add_cores(keep, send)
    resid = wide(x_own) + wide(here) + wide(swap_xh(there))
    resid_low = narrow(resid)
    mlp_blocks = gather_two(mlp_shard, (r_one,))
    h_other, opposite = gather_other(resid_low)
    h_self = gather_own(resid_low, opposite)
    r_two, n, cot, act, dgu, keep, send = mlp(
        table, other_at, (*h_other, *h_self), (*cot_other, *cot_self), gains, mlp_blocks
    )
    sums = add_cores(keep, send)
    mlp_terms = grads_mlp(table, dgu, act, n, cot, sums[:1])
    d_normed_two = sum_terms(spread_eight(sums[2], sums[3], sums[0], sums[1]))
    mlp_terms = tie(mlp_terms, d_normed_two)
    keep, send = down(table, other_at, act, mlp_blocks, (d_normed_two,))
    (opposite,) = tie((swap_xh(d_normed_two),), keep)
    keep, send = tie((keep, send), opposite)
    d_normed_all = gather_own(d_normed_two, opposite)
    mlp_terms = reduce_start(mlp_terms, ())
    away, second, own = add_cores_paired(keep, send)
    passed = cross(False)(away)
    mlp_out = own, (passed, 0), cross(True)(add_two(second, (passed, 1)))
    d_resid, keep, send, *attn_terms = attention_back(
        table,
        d_normed_all,
        h_self,
        cot_self,
        r_two,
        gains,
        q,
        k,
        v,
        o,
        cos,
        sin,
        normed_one,
        probs,
        attn_blocks,
        x_all,
        r_one,
        mlp_terms[:1],
    )
    here, there = add_cores(keep, send)

    d_normed_one = here, swap_xh(there)
    mlp_parts = reduce_end(*mlp_terms, ())
    attn_terms = reduce_start(attn_terms, (here, mlp_parts[0]))
    attn_parts = reduce_end(*attn_terms, d_normed_one[1:])
    mlp_total, mlp_pack = sum_pack(other_at, mlp_parts, attn_terms[:1])
    mixed, input_grad = outputs(
        resid, mlp_out, d_resid, d_normed_one, x_own, r_one, gains, attn_parts[:1]
    )
    attn_total, attn_pack = sum_pack(other_at, attn_parts, (mixed,))
    grad_gate, grad_up, grad_down, sum_two = finish_mlp(
        other_at, mlp_total, swap_xl(mlp_pack), w_gate, w_up
    )
    grad_query, grad_keyval, grad_output, sum_one = finish_attention(
        other_at, attn_total, swap_xl(attn_pack), w_query, key_value_weight
    )
    sums = jnp.concatenate([sum_one, sum_two], 0).reshape(1, 128)
    sums = (sums + swap_core(sums) + swap_xh(sums) + swap_both(sums)).reshape(2, 64)
    gain_one = sums[0] / wide(gain_attention)
    gain_two = sums[1] / wide(gain_mlp)
    return (
        mixed,
        input_grad,
        grad_query,
        grad_keyval,
        grad_output.T,
        grad_gate,
        grad_up,
        grad_down.T,
        gain_one,
        gain_two,
    )


def solution(mesh):
    fine = Mesh(mesh.devices.reshape(SIZES), AXES)
    both, turned, rows = P(ROW, COL), P(COL, ROW), P(ROW)
    return jax.shard_map(
        shards,
        mesh=fine,
        in_specs=(both, both, both, turned, both, both, turned, rows, rows, rows, rows, both),
        out_specs=(both, both, both, both, turned, both, both, turned, rows, rows),
        check_vma=False,
    )
```
